128 devices in a mesh: grp: 4 (over x), patch: 32 (over y, z, core).
Axes of the slice: x: 4, y: 4, z: 4, core: 2. Of those that a mesh axis runs over, the one named last changes fastest.
Arguments:
- strip_latent: bfloat16 [32768, 512], P(('grp', 'patch')), may hold values from -6 to 6
- strip_owner: int32 [32768, 1], P(('grp', 'patch')), may hold values from 0 to 127; in each aligned block of 256 rows (0 to 255, 256 to 511, ...) at most 8 rows name the same one
- strip_node: int32 [32768], P(('grp', 'patch')), may hold values from 0 to 4095
- dec_first: bfloat16 [512, 512], replicated, may hold values from -0.25 to 0.25
- dec_second: bfloat16 [512, 512], replicated, may hold values from -0.25 to 0.25
- grid_feats: bfloat16 [524288, 512], P(('grp', 'patch')), may hold values from -6 to 6
- g2m_target: int32 [524288], P(('grp', 'patch')), may hold values from 0 to 1535, as said below
- enc_first: bfloat16 [512, 512], replicated, may hold values from -0.25 to 0.25
- enc_second: bfloat16 [512, 512], replicated, may hold values from -0.25 to 0.25
- mesh_init: bfloat16 [65536, 512], P(('grp', 'patch')), may hold values from -6 to 6
- mesh_nbrs: int32 [65536, 6], P(('grp', 'patch')), may hold values from 0 to 639, as said below
- proc_self: bfloat16 [512, 512], replicated, may hold values from -0.25 to 0.25
- proc_agg: bfloat16 [512, 512], replicated, may hold values from -0.109375 to 0.109375
- proc_out: bfloat16 [512, 512], replicated, may hold values from -0.25 to 0.25
Outputs:
- mesh_out: bfloat16 [65536, 512], P(('grp', 'patch'))
The draws below stay inside these ranges and needn't reach their ends.
Inputs may be any that keep to these rules, and one draw needn't show every extreme that they name: `strip_owner`: among the rows of one device no owner is named more than 8 times, a bound that some block reaches. `g2m_target`: A value v names mesh node v % 512 of the patch before (v // 512 = 0), the own patch (1) or the patch after (2) in the same group; the first patch of a group never names the one before, the last never the one after. `mesh_nbrs`: as in the reference program; the first patch of a group never names e < 64, the last never e >= 576; repeated neighbours count as often as named.
All inputs are finite; a program needn't handle non-finite values.
Results may differ from the reference program's by a relative error of at most 0.008.
Values may be sent and summed in bfloat16 or wider, within the bound.
A program may use at most 64 MiB of HBM per device.

```python
import math
import jax
import jax.numpy as jnp
import numpy as np

D = 512
GN = 4096
MN = 512
BR = 256
CAP = 8
NB = 6
H = 64
BTOT = 32768
GTOT = 524288
MTOT = 65536
N_GRP = 4
N_PATCH = 32
DEVICES = 128


def draw_g2m_target(key, part):
    key = jax.random.fold_in(key, 11)
    values = jax.random.randint(key, (GTOT,), 0, 3 * MN, dtype=jnp.int32)
    patch_pos = jnp.arange(GTOT, dtype=jnp.int32) // GN % N_PATCH
    values = jnp.where((patch_pos == 0) & (values < MN), values + MN, values)
    values = jnp.where((patch_pos == N_PATCH - 1) & (values >= 2 * MN), values - MN, values)
    return values


def draw_mesh_nbrs(key, part):
    key = jax.random.fold_in(key, 23)
    values = jax.random.randint(key, (MTOT, NB), 0, MN + 2 * H, dtype=jnp.int32)
    patch_pos = (jnp.arange(MTOT, dtype=jnp.int32) // MN % N_PATCH)[:, None]
    values = jnp.where((patch_pos == 0) & (values < H), values + H, values)
    values = jnp.where((patch_pos == N_PATCH - 1) & (values >= H + MN), values - H, values)
    return values


def plant(drawn, rng, low, high):
    spot = [jax.random.randint(jax.random.fold_in(rng, axis), (), 0, length) for axis, length in enumerate(drawn.shape)]
    widest = drawn.shape.index(max(drawn.shape))
    next_to = spot[:widest] + [(spot[widest] + 1) % drawn.shape[widest]] + spot[widest + 1:]
    return drawn.at[tuple(spot)].set(low).at[tuple(next_to)].set(high)


def shard_levels(rng, shape, split, least, top_value):
    level = 1.0
    for dim, parts in split:
        draws = jax.random.uniform(jax.random.fold_in(jax.random.fold_in(rng, 6), dim), (parts,), jnp.float32, least / len(split), top_value / len(split))
        level = level * jnp.repeat(jnp.exp(draws), shape[dim] // parts).reshape((-1,) + (1,) * (len(shape) - 1 - dim))
    return level


def assign_block(key, own, number, rows, number_of, top, reach, slope):
    sequence = jax.random.permutation(key, number_of)
    crowded, common = load_shares(number_of, rows * top, reach, slope, True), load_shares(number_of, rows * top, reach, slope, False)
    places = jnp.arange(number_of)

    def named(lengths, turn):
        used = int((lengths > 0).sum())
        fixed = max(1, used // 4)
        moved = fixed + (places - fixed + turn * (used - fixed)) % max(1, number_of - fixed)
        return jnp.zeros((number_of,), jnp.int32).at[sequence[jnp.where(places < fixed, places, moved)]].set(jnp.asarray(lengths, jnp.int32))

    lengths = jnp.where(number % 4 == 0, named(crowded, number // 4), named(common, number - number // 4 - 1))
    mixed = jax.random.permutation(jax.random.fold_in(own, 3), number_of)
    donor, sink = mixed[0:number_of // 2 * 2:2], mixed[1:number_of // 2 * 2:2]
    slack = jnp.minimum(lengths[donor] - 1, reach - lengths[sink]) // 2
    slack = jnp.where((donor == sequence[0]) | (sink == sequence[0]) | (lengths[sink] == 0), 0, jnp.maximum(slack, 0))
    moved = jax.random.randint(jax.random.fold_in(own, 4), (number_of // 2,), 0, 1 << 20) % (slack + 1)
    lengths = lengths.at[donor].add(-moved).at[sink].add(moved)
    labels = jnp.searchsorted(jnp.cumsum(lengths), jnp.arange(rows * top), side="right").astype(jnp.int32)
    table = labels.reshape(top, rows).T
    table = table[jax.random.permutation(jax.random.fold_in(own, 1), rows)]
    turn = jax.random.randint(jax.random.fold_in(own, 2), (rows, 1), 0, top)
    return jnp.take_along_axis(table, (jnp.arange(top)[None, :] + turn) % top, axis=1)


def load_shares(amount, total, reach, slope, full):
    loads = [(1 << 20) // math.isqrt(grade ** slope) + 1 for grade in range(1, amount + 1)]
    largest = reach if full else min(reach, max(-(-total // amount), total * loads[0] // sum(loads)))
    least = 1 if total - largest >= amount - 1 else 0
    holding, spare = [largest] + [least] * (amount - 1), total - largest - least * (amount - 1)
    while spare > 0:
        movable = [i for i in range(1, amount) if holding[i] < largest] or [i for i in range(1, amount) if holding[i] < reach]
        mass, budget = sum([loads[i] for i in movable]), spare
        for i in movable:
            addition = min(reach - holding[i], max(1, budget * loads[i] // mass), spare)
            holding[i] = holding[i] + addition
            spare = spare - addition
    return np.array(holding)


def scatter_about(key, shape, scale, bound, split=(), kind=jnp.bfloat16):
    factor_of = shard_levels(key, shape, split, -0.22, 0.18) if split else 1.0
    drawn = jax.random.normal(key, shape, jnp.float32) * scale * factor_of
    return jnp.minimum(jnp.maximum(drawn, -bound), bound).astype(kind)


def setup_inputs(seed: int = 0) -> dict:
    seeds = jax.random.split(jax.random.key(seed), 15)
    strip_latent = scatter_about(seeds[0], (BTOT, D), 1.0, 6.0, ((0, 128),))
    strip_owner_keys = jax.random.split(jax.random.fold_in(seeds[1], 1), BTOT // BR)
    strip_owner_turns = jax.random.permutation(jax.random.fold_in(seeds[1], 3), BTOT // BR)
    strip_owner = jax.vmap(lambda own, number: assign_block(jax.random.fold_in(seeds[1], 2), own, number, BR, DEVICES, 1, CAP, 2))(strip_owner_keys, strip_owner_turns).reshape((BTOT, 1))
    strip_node = plant(jax.random.randint(seeds[2], (BTOT,), 0, GN), jax.random.fold_in(seeds[2], 1), 0, GN - 1).astype(jnp.int32)
    dec_first = scatter_about(seeds[3], (D, D), D ** -0.5, 0.25)
    dec_second = scatter_about(seeds[4], (D, D), D ** -0.5, 0.25)
    grid_feats = scatter_about(seeds[5], (GTOT, D), 1.0, 6.0, ((0, 128),))
    g2m_target = draw_g2m_target(jax.random.fold_in(seeds[14], 71), 0)
    enc_first = scatter_about(seeds[7], (D, D), D ** -0.5, 0.25)
    enc_second = scatter_about(seeds[8], (D, D), D ** -0.5, 0.25)
    mesh_init = scatter_about(seeds[9], (MTOT, D), 1.0, 6.0, ((0, 128),))
    mesh_nbrs = draw_mesh_nbrs(jax.random.fold_in(seeds[14], 71), 0)
    proc_self = scatter_about(seeds[11], (D, D), D ** -0.5, 0.25)
    proc_agg = scatter_about(seeds[12], (D, D), (NB * D) ** -0.5, 0.109375)
    proc_out = scatter_about(seeds[13], (D, D), D ** -0.5, 0.25)
    return {"strip_latent": strip_latent, "strip_owner": strip_owner, "strip_node": strip_node, "dec_first": dec_first, "dec_second": dec_second, "grid_feats": grid_feats, "g2m_target": g2m_target, "enc_first": enc_first, "enc_second": enc_second, "mesh_init": mesh_init, "mesh_nbrs": mesh_nbrs, "proc_self": proc_self, "proc_agg": proc_agg, "proc_out": proc_out}


def two_layer(inputs, first, second):
    hidden = jax.nn.silu(jnp.dot(inputs, first, preferred_element_type=jnp.float32)).astype(jnp.bfloat16)
    return jnp.dot(hidden, second, preferred_element_type=jnp.float32).astype(jnp.bfloat16)


def reference(strip_latent, strip_owner, strip_node, dec_first, dec_second, grid_feats, g2m_target, enc_first, enc_second, mesh_init, mesh_nbrs, proc_self, proc_agg, proc_out):
    devices = N_GRP * N_PATCH
    boundary = two_layer(strip_latent, dec_first, dec_second)
    target_rows = (strip_owner[:, 0] * GN + strip_node).astype(jnp.int32)
    forcing = jax.ops.segment_sum(boundary.astype(jnp.float32), target_rows, num_segments=GTOT)
    grid_in = (grid_feats.astype(jnp.float32) + forcing).astype(jnp.bfloat16)
    messages = two_layer(grid_in, enc_first, enc_second)
    owner_dev = jnp.arange(GTOT, dtype=jnp.int32) // GN
    mesh_rows = ((owner_dev + g2m_target // MN - 1) * MN + g2m_target % MN).astype(jnp.int32)
    summed = jax.ops.segment_sum(messages.astype(jnp.float32), mesh_rows, num_segments=MTOT)
    mesh_lat = (mesh_init.astype(jnp.float32) + summed).astype(jnp.bfloat16)
    blocks = mesh_lat.reshape(N_GRP, N_PATCH, MN, D)
    empty = jnp.zeros((N_GRP, 1, H, D), jnp.bfloat16)
    before = jnp.concatenate([empty, blocks[:, :-1, MN - H:]], axis=1)
    after = jnp.concatenate([blocks[:, 1:, :H], empty], axis=1)
    extended = jnp.concatenate([before, blocks, after], axis=2).reshape(devices * (MN + 2 * H), D)
    base = (jnp.arange(MTOT, dtype=jnp.int32) // MN) * (MN + 2 * H)
    agg = jnp.zeros((MTOT, D), jnp.float32)
    for slot in range(NB):
        agg = agg + extended[(base + mesh_nbrs[:, slot]).astype(jnp.int32)].astype(jnp.float32)
    agg = agg.astype(jnp.bfloat16)
    pre = jnp.dot(mesh_lat, proc_self, preferred_element_type=jnp.float32) + jnp.dot(agg, proc_agg, preferred_element_type=jnp.float32)
    proc_hidden = jax.nn.silu(pre).astype(jnp.bfloat16)
    update = jnp.dot(proc_hidden, proc_out, preferred_element_type=jnp.float32)
    return (mesh_lat.astype(jnp.float32) + update).astype(jnp.bfloat16)
```

```python
import jax
import jax.numpy as jnp
from jax import lax
from jax.experimental import pallas as pl
from jax.experimental.pallas import tpu as pltpu
from jax.sharding import PartitionSpec as P

CAP = 8
NB = 6
H = 64
D = 512
GN = 4096
MN = 512
BR = 256
NDEV = 128
SLOTS = NDEV * CAP
CHUNK = 512
NCHUNK = GN // CHUNK
BLK = 256
MESH = pl.DeviceIdType.MESH
F32 = jnp.float32
BF16 = jnp.bfloat16

ORDER = sorted(
    [
        (dx, dy, dz, dc)
        for dx in range(4)
        for dy in range(4)
        for dz in range(4)
        for dc in range(2)
        if dx or dy or dz or dc
    ],
    key=lambda o: (-sum(min(v, 4 - v) for v in o[:3]), (o[0] + 2 * o[1] + 3 * o[2]) % 4, o),
)


def coords():
    g = lax.axis_index("grp")
    p = lax.axis_index("patch")
    return g, p // 8, (p // 2) % 4, p % 2


def shifted(at, offset):
    x, y, z, c = at
    dx, dy, dz, dc = offset
    xx = (x + dx) % 4 if dx else x
    yy = (y + dy) % 4 if dy else y
    zz = (z + dz) % 4 if dz else z
    cc = 1 - c if dc else c
    return xx, yy * 8 + zz * 2 + cc


def silu(v):
    half = v * 0.5
    return half + half * jnp.tanh(half)


def dot(a, b):
    return jnp.dot(a, b, preferred_element_type=F32)


def iota(shape, dim):
    return lax.broadcasted_iota(jnp.int32, shape, dim)


def onehot(mask):
    return jnp.where(mask, 1.0, 0.0).astype(BF16)


def col_to_row(col):
    n = col.shape[0]
    parts = []
    for b in range(n // 128):
        diag = iota((128, 128), 0) == iota((128, 128), 1)
        parts.append(
            jnp.sum(jnp.where(diag, col[b * 128 : (b + 1) * 128], 0.0), axis=0, keepdims=True)
        )
    return jnp.concatenate(parts, axis=1)


def kernel(
    strip, owner, node, d1, d2, feats, tgt, e1, e2, init, nbrs, ps, pa, po,
    out,
    strip_v, owner_v, node_v, d1_v, d2_v, feats_v, tgt_v, e1_v, e2_v, init_v, nbrs_v, ps_v, pa_v, po_v,
    send, nsend, recv, nrecv, sums, g, uj, hj, eq, tp, delta, xs, xr, hr, lat, c_own, c_halo,
    lsem, fsem, s_row, r_row, s_node, r_node, s_x, r_x, s_h, r_h, bar_x, bar_y, own_sem,
):
    at = coords()
    gi = lax.axis_index("grp")
    pi = lax.axis_index("patch")
    me = gi * 32 + pi

    loads = [
        pltpu.make_async_copy(src, dst, lsem.at[i])
        for i, (src, dst) in enumerate(
            [
                (owner, owner_v), (node, node_v), (strip, strip_v), (d1, d1_v), (d2, d2_v),
                (e1, e1_v), (tgt, tgt_v), (nbrs, nbrs_v), (init, init_v), (e2, e2_v),
                (ps, ps_v), (pa, pa_v), (po, po_v),
            ]
        )
    ]

    def feat_load(c):
        rows = pl.ds(pl.multiple_of(c * CHUNK, CHUNK), CHUNK)
        return pltpu.make_async_copy(feats.at[rows], feats_v.at[rows], fsem.at[c])

    barrier = pltpu.get_barrier_semaphore()
    plane = [(0, 0, dz, dc) for dz in range(4) for dc in range(2) if dz or dc]
    xline = [(dx, 0, 0, 0) for dx in (1, 2, 3)]
    yline = [(0, dy, 0, 0) for dy in (1, 2, 3)]
    for o in plane + xline + yline:
        pl.semaphore_signal(barrier, inc=1, device_id=shifted(at, o), device_id_type=MESH)

    for c in loads[:6]:
        c.start()
    for c in range(NCHUNK):
        feat_load(c).start()
    for c in loads[6:]:
        c.start()

    loads[0].wait()
    loads[1].wait()
    owner_row = col_to_row(owner_v[...].astype(F32)).astype(jnp.int32)
    node_row = jnp.concatenate([node_v[0:1, :], node_v[1:2, :]], axis=1).astype(F32)
    hit = iota((NDEV, BR), 0) == owner_row
    upper = onehot(iota((BR, BR), 0) < iota((BR, BR), 1))
    before = dot(onehot(hit), upper)
    slot_row = jnp.sum(jnp.where(hit, before, 0.0), axis=0, keepdims=True).astype(jnp.int32)
    pos_row = owner_row * CAP + slot_row
    placed = iota((SLOTS, BR), 0) == pos_row
    ncol = jnp.sum(jnp.where(placed, node_row + 1.0, 0.0), axis=1, keepdims=True) - 1.0
    ncol = jnp.broadcast_to(ncol.reshape(NDEV, CAP, 1), (NDEV, CAP, 128))
    pick = iota((NDEV, CAP, 128), 1) == iota((NDEV, CAP, 128), 2)
    nsend[...] = jnp.sum(jnp.where(pick, ncol, 0.0), axis=1, keepdims=True)

    pl.semaphore_wait(barrier, len(plane + xline + yline))
    for o in xline:
        pl.semaphore_signal(bar_x, inc=1, device_id=shifted(at, o), device_id_type=MESH)

    for c in loads[2:6]:
        c.wait()
    hid = silu(dot(strip_v[...], d1_v[...])).astype(BF16)
    bnd = dot(hid, d2_v[...]).astype(BF16)
    rows_out = dot(bnd, e1_v[...]).astype(BF16)
    send[...] = dot(onehot(placed), rows_out).astype(BF16).reshape(NDEV, CAP, D)

    pl.semaphore_wait(bar_x, 3)
    for o in yline:
        pl.semaphore_signal(bar_y, inc=1, device_id=shifted(at, o), device_id_type=MESH)
    pl.semaphore_wait(bar_y, 3)

    for o in ORDER:
        to = shifted(at, o)
        idx = to[0] * 32 + to[1]
        pltpu.make_async_remote_copy(
            src_ref=nsend.at[idx], dst_ref=nrecv.at[me], send_sem=s_node, recv_sem=r_node,
            device_id=to, device_id_type=MESH,
        ).start()
    for o in ORDER:
        to = shifted(at, o)
        idx = to[0] * 32 + to[1]
        pltpu.make_async_remote_copy(
            src_ref=send.at[idx], dst_ref=recv.at[me], send_sem=s_row, recv_sem=r_row,
            device_id=to, device_id_type=MESH,
        ).start()
    own_n = pltpu.make_async_copy(nsend.at[me], nrecv.at[me], own_sem.at[0])
    own_r = pltpu.make_async_copy(send.at[me], recv.at[me], own_sem.at[1])
    own_n.start()
    own_r.start()

    for c in loads[6:]:
        c.wait()
    sums[...] = jnp.zeros_like(sums)

    def encode(c, _):
        feat_load(c).wait()
        rows = pl.ds(pl.multiple_of(c * CHUNK, CHUNK), CHUNK)
        h = silu(dot(feats_v[rows, :], e1_v[...])).astype(BF16)
        t = tgt_v[pl.ds(pl.multiple_of(c * (CHUNK // 128), CHUNK // 128), CHUNK // 128), :]
        t_row = jnp.concatenate([t[i : i + 1, :] for i in range(CHUNK // 128)], axis=1)
        for b in range(3):
            hot = onehot(iota((MN, CHUNK), 0) + b * MN == t_row)
            sums[b * MN : (b + 1) * MN, :] += dot(hot, h)
        return 0

    lax.fori_loop(0, NCHUNK, encode, 0)

    halo_lane = iota((MN, 2 * H), 1)
    halo_name = jnp.where(halo_lane < H, halo_lane, halo_lane + MN)
    own_name = iota((MN, MN), 1) + H
    own_cnt = jnp.zeros((MN, MN), F32)
    halo_cnt = jnp.zeros((MN, 2 * H), F32)
    for k in range(NB):
        e = nbrs_v[:, k : k + 1]
        own_cnt += jnp.where(e == own_name, 1.0, 0.0)
        halo_cnt += jnp.where(e == halo_name, 1.0, 0.0)
    c_own[...] = own_cnt.astype(BF16)
    c_halo[...] = halo_cnt.astype(BF16)

    all_n = pltpu.make_async_remote_copy(
        src_ref=nsend.at[pl.ds(0, NDEV - 1)], dst_ref=nrecv.at[pl.ds(0, NDEV - 1)],
        send_sem=s_node, recv_sem=r_node, device_id=(gi, pi), device_id_type=MESH,
    )
    all_n.wait_send()
    all_n.wait_recv()
    own_n.wait()
    got = jnp.broadcast_to(nrecv[...], (NDEV, CAP, 128))
    node_col = jnp.sum(jnp.where(pick, got, 0.0), axis=2, keepdims=True).reshape(SLOTS, 1)
    nrow = col_to_row(node_col)
    same = node_col == nrow
    eq[...] = onehot(same)
    earlier = iota((SLOTS, SLOTS), 0) < iota((SLOTS, SLOTS), 1)
    dup = jnp.sum(jnp.where(same & earlier, 1.0, 0.0), axis=0, keepdims=True)

    node_int = node_col.astype(jnp.int32)
    g[...] = jnp.zeros_like(g)

    def gather(c, _):
        rows = pl.ds(pl.multiple_of(c * CHUNK, CHUNK), CHUNK)
        hot = onehot(iota((SLOTS, CHUNK), 1) + c * CHUNK == node_int)
        g[...] += dot(hot, feats_v[rows, :])
        return 0

    lax.fori_loop(0, NCHUNK, gather, 0)
    u = dot(g[...].astype(BF16), e1_v[...])
    uj[...] = u
    hj[...] = silu(u)

    hi_hot = onehot(iota((SLOTS, GN // 128), 1) == node_int // 128)
    t_all = tgt_v[...]
    t_hi = dot(hi_hot, (t_all // 64).astype(F32).astype(BF16))
    t_lo = dot(hi_hot, (t_all % 64).astype(F32).astype(BF16))
    t_val = t_hi * 64.0 + t_lo
    lane_pick = iota((SLOTS, 128), 1) == node_int % 128
    t_col = jnp.sum(jnp.where(lane_pick, t_val, 0.0), axis=1, keepdims=True)
    t_row = col_to_row(t_col)
    t_row = jnp.where((dup == 0.0) & (nrow >= 0.0), t_row, -1.0).astype(jnp.int32)
    for b in range(3):
        tp[b * MN : (b + 1) * MN, :] = onehot(iota((MN, SLOTS), 0) + b * MN == t_row)

    all_r = pltpu.make_async_remote_copy(
        src_ref=send.at[pl.ds(0, NDEV - 1)], dst_ref=recv.at[pl.ds(0, NDEV - 1)],
        send_sem=s_row, recv_sem=r_row, device_id=(gi, pi), device_id_type=MESH,
    )
    all_r.wait_send()
    all_r.wait_recv()
    own_r.wait()
    f = dot(eq[...], recv[...].reshape(SLOTS, D))
    delta[...] = (silu(uj[...] + f) - hj[...]).astype(BF16)

    up = (gi, (pi + 1) % 32)
    down = (gi, (pi + 31) % 32)
    copies = []
    for b in range(MN // BLK):
        for side, base, to in ((0, 2 * MN, up), (1, 0, down)):
            rows = slice(base + b * BLK, base + (b + 1) * BLK)
            part = pl.ds(b * BLK, BLK)
            xs[side, part, :] = (sums[rows, :] + dot(tp[rows, :], delta[...])).astype(BF16)
            i = 2 * b + side
            c = pltpu.make_async_remote_copy(
                src_ref=xs.at[side, part], dst_ref=xr.at[side, part],
                send_sem=s_x.at[i], recv_sem=r_x.at[i], device_id=to, device_id_type=MESH,
            )
            c.start()
            copies.append(c)
    sums[MN : 2 * MN, :] += dot(tp[MN : 2 * MN, :], delta[...])

    halo = [
        pltpu.make_async_remote_copy(
            src_ref=lat.at[pl.ds(src, H)], dst_ref=hr.at[pl.ds(dst, H)],
            send_sem=s_h.at[i], recv_sem=r_h.at[i], device_id=to, device_id_type=MESH,
        )
        for i, (src, dst, to) in enumerate(((0, H, down), (MN - H, 0, up)))
    ]
    for b in range(MN // BLK):
        copies[2 * b].wait_recv()
        copies[2 * b + 1].wait_recv()
        part = slice(b * BLK, (b + 1) * BLK)
        total = (
            sums[MN + b * BLK : MN + (b + 1) * BLK, :]
            + xr[0, part, :].astype(F32)
            + xr[1, part, :].astype(F32)
        ).astype(BF16)
        lat[part, :] = (init_v[part, :].astype(F32) + dot(total, e2_v[...])).astype(BF16)
        halo[b].start()

    pre = dot(lat[...], ps_v[...])
    agg = dot(c_own[...], lat[...])
    for c in halo:
        c.wait_recv()
    agg = (agg + dot(c_halo[...], hr[...])).astype(BF16)
    ph = silu(pre + dot(agg, pa_v[...])).astype(BF16)
    out[...] = (lat[...].astype(F32) + dot(ph, po_v[...])).astype(BF16)
    for c in copies + halo:
        c.wait_send()


def per_device(strip, owner, node, d1, d2, feats, tgt, e1, e2, init, nbrs, ps, pa, po):
    any_spec = pl.BlockSpec(memory_space=pl.ANY)
    weight = pltpu.VMEM((D, D), BF16)
    dma = pltpu.SemaphoreType.DMA
    return pl.pallas_call(
        kernel,
        out_shape=jax.ShapeDtypeStruct((MN, D), BF16),
        in_specs=[any_spec] * 14,
        out_specs=pl.BlockSpec(memory_space=pltpu.VMEM),
        scratch_shapes=[
            pltpu.VMEM((BR, D), BF16),
            pltpu.VMEM((BR, 1), jnp.int32),
            pltpu.VMEM((BR // 128, 128), jnp.int32),
            weight,
            weight,
            pltpu.VMEM((GN, D), BF16),
            pltpu.VMEM((GN // 128, 128), jnp.int32),
            weight,
            weight,
            pltpu.VMEM((MN, D), BF16),
            pltpu.VMEM((MN, NB), jnp.int32),
            weight,
            weight,
            weight,
            pltpu.VMEM((NDEV, CAP, D), BF16),
            pltpu.VMEM((NDEV, 1, 128), F32),
            pltpu.VMEM((NDEV, CAP, D), BF16),
            pltpu.VMEM((NDEV, 1, 128), F32),
            pltpu.VMEM((3 * MN, D), F32),
            pltpu.VMEM((SLOTS, D), F32),
            pltpu.VMEM((SLOTS, D), F32),
            pltpu.VMEM((SLOTS, D), F32),
            pltpu.VMEM((SLOTS, SLOTS), BF16),
            pltpu.VMEM((3 * MN, SLOTS), BF16),
            pltpu.VMEM((SLOTS, D), BF16),
            pltpu.VMEM((2, MN, D), BF16),
            pltpu.VMEM((2, MN, D), BF16),
            pltpu.VMEM((2 * H, D), BF16),
            pltpu.VMEM((MN, D), BF16),
            pltpu.VMEM((MN, MN), BF16),
            pltpu.VMEM((MN, 2 * H), BF16),
            dma((13,)),
            dma((NCHUNK,)),
            dma,
            dma,
            dma,
            dma,
            dma((2 * MN // BLK,)),
            dma((2 * MN // BLK,)),
            dma((2,)),
            dma((2,)),
            pltpu.SemaphoreType.REGULAR,
            pltpu.SemaphoreType.REGULAR,
            dma((2,)),
        ],
        compiler_params=pltpu.CompilerParams(
            collective_id=0, has_side_effects=True, vmem_limit_bytes=56 * 1024 * 1024
        ),
        name="fused",
    )(
        strip, owner, node.reshape(BR // 128, 128), d1, d2, feats, tgt.reshape(GN // 128, 128),
        e1, e2, init, nbrs, ps, pa, po,
    )


def solution(mesh):
    rows = P(("grp", "patch"), None)
    flat = P(("grp", "patch"))
    in_specs = (rows, rows, flat, P(), P(), rows, flat, P(), P(), rows, rows, P(), P(), P())
    return jax.shard_map(
        per_device, mesh=mesh, in_specs=in_specs, out_specs=rows, check_vma=False
    )
```

```python
import jax
import jax.numpy as jnp
from jax import lax
from jax.experimental import pallas as pl
from jax.experimental.pallas import tpu as pltpu
from jax.sharding import PartitionSpec as P

CAP = 8
NB = 6
H = 64
D = 512
GN = 4096
MN = 512
BR = 256
NDEV = 128
SLOTS = NDEV * CAP
CHUNK = 2048
NCHUNK = GN // CHUNK
HALF = 256
RUNS = ((0, 0, H), (MN - H, H, H), (H, 2 * H, MN - 2 * H))
PIECES = ((0, 2 * H), (2 * H, 320), (320, MN))
MESH = pl.DeviceIdType.MESH
F32 = jnp.float32
BF16 = jnp.bfloat16

ORDER = sorted(
    [
        (dx, dy, dz, dc)
        for dx in range(4)
        for dy in range(4)
        for dz in range(4)
        for dc in range(2)
        if dx or dy or dz or dc
    ],
    key=lambda o: (-sum(min(v, 4 - v) for v in o[:3]), (o[0] + 2 * o[1] + 3 * o[2]) % 4, o),
)


def coords():
    g = lax.axis_index("grp")
    p = lax.axis_index("patch")
    return g, p // 8, (p // 2) % 4, p % 2


def shifted(at, offset):
    x, y, z, c = at
    dx, dy, dz, dc = offset
    xx = (x + dx) % 4 if dx else x
    yy = (y + dy) % 4 if dy else y
    zz = (z + dz) % 4 if dz else z
    cc = 1 - c if dc else c
    return xx, yy * 8 + zz * 2 + cc


def silu(v):
    half = v * 0.5
    return half + half * jnp.tanh(half)


def dot(a, b):
    return jnp.dot(a, b, preferred_element_type=F32)


def iota(shape, dim):
    return lax.broadcasted_iota(jnp.int32, shape, dim)


def onehot(mask):
    return jnp.where(mask, 1.0, 0.0).astype(BF16)


def col_to_row(col):
    n = col.shape[0]
    parts = []
    for b in range(n // 128):
        diag = iota((128, 128), 0) == iota((128, 128), 1)
        parts.append(
            jnp.sum(jnp.where(diag, col[b * 128 : (b + 1) * 128], 0.0), axis=0, keepdims=True)
        )
    return jnp.concatenate(parts, axis=1)


def kernel(
    strip, owner, node, d1, d2, feats, tgt, e1, e2, init, nbrs, ps, pa, po,
    out,
    strip_v, owner_v, node_v, d1_v, d2_v, feats_v, tgt_v, e1_v, e2_v, init_v, nbrs_v, ps_v, pa_v, po_v,
    send, nsend, recv, nrecv, sums, uj, hj, eq, tp, delta, xs, xr, hr, lat, c_own, c_halo,
    lsem, fsem, s_row, r_row, s_node, r_node, s_x, r_x, s_h, r_h, own_sem,
):
    at = coords()
    gi = lax.axis_index("grp")
    pi = lax.axis_index("patch")
    me = gi * 32 + pi

    loads = [
        pltpu.make_async_copy(src, dst, lsem.at[i])
        for i, (src, dst) in enumerate(
            [
                (owner, owner_v), (node, node_v), (strip, strip_v), (d1, d1_v), (d2, d2_v),
                (e1, e1_v), (tgt, tgt_v), (nbrs, nbrs_v), (e2, e2_v), (ps, ps_v), (pa, pa_v), (po, po_v),
            ]
            + [(init.at[pl.ds(src, n)], init_v.at[pl.ds(dst, n)]) for src, dst, n in RUNS]
        )
    ]

    def feat_load(c):
        rows = pl.ds(pl.multiple_of(c * CHUNK, CHUNK), CHUNK)
        return pltpu.make_async_copy(feats.at[rows], feats_v.at[rows], fsem.at[c])

    for c in loads[:6]:
        c.start()
    barrier = pltpu.get_barrier_semaphore()
    for o in ORDER:
        pl.semaphore_signal(barrier, inc=1, device_id=shifted(at, o), device_id_type=MESH)
    for c in range(NCHUNK):
        feat_load(c).start()
    for c in loads[6:]:
        c.start()

    loads[0].wait()
    loads[1].wait()
    owner_row = owner_v[...]
    node_row = jnp.concatenate([node_v[0:1, :], node_v[1:2, :]], axis=1).astype(F32)
    hit = iota((NDEV, BR), 0) == owner_row
    upper = onehot(iota((BR, BR), 0) < iota((BR, BR), 1))
    before = dot(onehot(hit), upper)
    slot_row = jnp.sum(jnp.where(hit, before, 0.0), axis=0, keepdims=True).astype(jnp.int32)
    pos_row = owner_row * CAP + slot_row
    placed = iota((SLOTS, BR), 0) == pos_row
    ncol = jnp.sum(jnp.where(placed, node_row + 1.0, 0.0), axis=1, keepdims=True) - 1.0
    ncol = jnp.broadcast_to(ncol.reshape(NDEV, CAP, 1), (NDEV, CAP, 128))
    pick = iota((NDEV, CAP, 128), 1) == iota((NDEV, CAP, 128), 2)
    nsend[...] = jnp.sum(jnp.where(pick, ncol, 0.0), axis=1, keepdims=True)

    for c in loads[2:6]:
        c.wait()
    hid = silu(dot(strip_v[...], d1_v[...])).astype(BF16)
    bnd = dot(hid, d2_v[...]).astype(BF16)
    rows_out = dot(bnd, e1_v[...]).astype(BF16)
    send[...] = dot(onehot(placed), rows_out).astype(BF16).reshape(NDEV, CAP, D)

    pl.semaphore_wait(barrier, NDEV - 1)
    for o in ORDER:
        to = shifted(at, o)
        idx = to[0] * 32 + to[1]
        pltpu.make_async_remote_copy(
            src_ref=nsend.at[idx], dst_ref=nrecv.at[me], send_sem=s_node, recv_sem=r_node,
            device_id=to, device_id_type=MESH,
        ).start()
    for o in ORDER:
        to = shifted(at, o)
        idx = to[0] * 32 + to[1]
        pltpu.make_async_remote_copy(
            src_ref=send.at[idx], dst_ref=recv.at[me], send_sem=s_row, recv_sem=r_row,
            device_id=to, device_id_type=MESH,
        ).start()
    own_n = pltpu.make_async_copy(nsend.at[me], nrecv.at[me], own_sem.at[0])
    own_r = pltpu.make_async_copy(send.at[me], recv.at[me], own_sem.at[1])
    own_n.start()
    own_r.start()

    for c in loads[6:]:
        c.wait()
    t_all = tgt_v[...]
    t_side, t_mesh = t_all // MN, t_all % MN
    t_mesh = jnp.where(
        t_mesh < H, t_mesh, jnp.where(t_mesh >= MN - H, t_mesh - (MN - 2 * H), t_mesh + H)
    )
    t_all = t_side * MN + t_mesh
    tgt_v[...] = t_all
    sums[...] = jnp.zeros_like(sums)

    def encode(c, _):
        feat_load(c).wait()
        rows = pl.ds(pl.multiple_of(c * CHUNK, CHUNK), CHUNK)
        h = silu(dot(feats_v[rows, :], e1_v[...])).astype(BF16)
        t = tgt_v[pl.ds(pl.multiple_of(c * (CHUNK // 128), CHUNK // 128), CHUNK // 128), :]
        t_row = jnp.concatenate([t[i : i + 1, :] for i in range(CHUNK // 128)], axis=1)
        for b in range(3):
            hot = onehot(iota((MN, CHUNK), 0) + b * MN == t_row)
            sums[b * MN : (b + 1) * MN, :] += dot(hot, h)
        return 0

    lax.fori_loop(0, NCHUNK, encode, 0)

    halo_lane = iota((MN, 2 * H), 1)
    halo_name = jnp.where(halo_lane < H, halo_lane, halo_lane + MN)
    lane = iota((MN, MN), 1)
    own_name = jnp.where(lane < H, lane + H, jnp.where(lane < 2 * H, lane + MN - H, lane))
    own_cnt = jnp.zeros((MN, MN), F32)
    halo_cnt = jnp.zeros((MN, 2 * H), F32)
    names = jnp.concatenate([nbrs_v[...].astype(F32), jnp.zeros((8 - NB, MN), F32)], axis=0)
    names = names.T.astype(jnp.int32)
    names = jnp.concatenate([names[src : src + n] for src, _, n in RUNS], axis=0)
    for k in range(NB):
        e = names[:, k : k + 1]
        own_cnt += jnp.where(e == own_name, 1.0, 0.0)
        halo_cnt += jnp.where(e == halo_name, 1.0, 0.0)
    c_own[...] = own_cnt.astype(BF16)
    c_halo[...] = halo_cnt.astype(BF16)

    all_n = pltpu.make_async_remote_copy(
        src_ref=nsend.at[pl.ds(0, NDEV - 1)], dst_ref=nrecv.at[pl.ds(0, NDEV - 1)],
        send_sem=s_node, recv_sem=r_node, device_id=(gi, pi), device_id_type=MESH,
    )
    all_n.wait_send()
    all_n.wait_recv()
    own_n.wait()
    got = jnp.broadcast_to(nrecv[...], (NDEV, CAP, 128))
    node_col = jnp.sum(jnp.where(pick, got, 0.0), axis=2, keepdims=True).reshape(SLOTS, 1)
    nrow = col_to_row(node_col)
    same = node_col == nrow
    eq[...] = onehot(same)
    earlier = iota((SLOTS, SLOTS), 0) < iota((SLOTS, SLOTS), 1)
    dup = jnp.sum(jnp.where(same & earlier, 1.0, 0.0), axis=0, keepdims=True)

    node_int = node_col.astype(jnp.int32)
    picked = jnp.zeros((SLOTS, D), F32)
    for c in range(NCHUNK):
        hot = onehot(iota((SLOTS, CHUNK), 1) + c * CHUNK == node_int)
        picked = picked + dot(hot, feats_v[c * CHUNK : (c + 1) * CHUNK, :])
    u = dot(picked.astype(BF16), e1_v[...])
    uj[...] = u
    hj[...] = silu(u)

    hi_hot = onehot(iota((SLOTS, GN // 128), 1) == node_int // 128)
    t_hi = dot(hi_hot, (t_all // 64).astype(F32).astype(BF16))
    t_lo = dot(hi_hot, (t_all % 64).astype(F32).astype(BF16))
    t_val = t_hi * 64.0 + t_lo
    lane_pick = iota((SLOTS, 128), 1) == node_int % 128
    t_col = jnp.sum(jnp.where(lane_pick, t_val, 0.0), axis=1, keepdims=True)
    t_row = col_to_row(t_col)
    t_row = jnp.where((dup == 0.0) & (nrow >= 0.0), t_row, -1.0).astype(jnp.int32)
    for b in range(3):
        tp[b * MN : (b + 1) * MN, :] = onehot(iota((MN, SLOTS), 0) + b * MN == t_row)

    all_r = pltpu.make_async_remote_copy(
        src_ref=send.at[pl.ds(0, NDEV - 1)], dst_ref=recv.at[pl.ds(0, NDEV - 1)],
        send_sem=s_row, recv_sem=r_row, device_id=(gi, pi), device_id_type=MESH,
    )
    all_r.wait_send()
    all_r.wait_recv()
    own_r.wait()
    up = (gi, (pi + 1) % 32)
    down = (gi, (pi + 31) % 32)
    copies = {}

    def send_sums(w, b):
        cols = slice(w * HALF, (w + 1) * HALF)
        lo, hi = PIECES[b]
        part = pl.ds(lo, hi - lo)
        for side, base, to in ((0, 2 * MN, up), (1, 0, down)):
            rows = slice(base + lo, base + hi)
            xs[side, w, part, :] = (sums[rows, cols] + dot(tp[rows, :], delta[:, cols])).astype(BF16)
            i = (w * len(PIECES) + b) * 2 + side
            c = pltpu.make_async_remote_copy(
                src_ref=xs.at[side, w, part], dst_ref=xr.at[side, w, part],
                send_sem=s_x.at[i], recv_sem=r_x.at[i], device_id=to, device_id_type=MESH,
            )
            c.start()
            copies[w, b, side] = c

    for w in range(D // HALF):
        cols = slice(w * HALF, (w + 1) * HALF)
        f = dot(eq[...], recv[:, :, cols].reshape(SLOTS, HALF))
        delta[:, cols] = (silu(uj[:, cols] + f) - hj[:, cols]).astype(BF16)
        send_sums(w, 0)
    for b in range(1, len(PIECES)):
        for w in range(D // HALF):
            send_sums(w, b)
    sums[MN : 2 * MN, :] += dot(tp[MN : 2 * MN, :], delta[...])

    halo = [
        pltpu.make_async_remote_copy(
            src_ref=lat.at[pl.ds(src, H)], dst_ref=hr.at[pl.ds(dst, H)],
            send_sem=s_h.at[i], recv_sem=r_h.at[i], device_id=to, device_id_type=MESH,
        )
        for i, (src, dst, to) in enumerate(((0, H, down), (H, 0, up)))
    ]
    agg = jnp.zeros((MN, D), F32)
    pre = []
    for b, (lo, hi) in enumerate(PIECES):
        for w in range(D // HALF):
            for side in range(2):
                copies[w, b, side].wait_recv()
        total = [
            (
                sums[MN + lo : MN + hi, w * HALF : (w + 1) * HALF]
                + xr[0, w, lo:hi, :].astype(F32)
                + xr[1, w, lo:hi, :].astype(F32)
            ).astype(BF16)
            for w in range(D // HALF)
        ]
        now = (
            init_v[lo:hi, :].astype(F32) + dot(jnp.concatenate(total, axis=1), e2_v[...])
        ).astype(BF16)
        lat[lo:hi, :] = now
        if b == 0:
            for c in halo:
                c.start()
        pre.append(dot(now, ps_v[...]))
        agg = agg + dot(c_own[:, lo:hi], now)
    for c in halo:
        c.wait_recv()
    agg = (agg + dot(c_halo[...], hr[...])).astype(BF16)
    hidden = silu(jnp.concatenate(pre, axis=0) + dot(agg, pa_v[...])).astype(BF16)
    new = (lat[...].astype(F32) + dot(hidden, po_v[...])).astype(BF16)
    for src, dst, n in RUNS:
        out[src : src + n, :] = new[dst : dst + n]
    for c in list(copies.values()) + halo:
        c.wait_send()


def per_device(strip, owner, node, d1, d2, feats, tgt, e1, e2, init, nbrs, ps, pa, po):
    any_spec = pl.BlockSpec(memory_space=pl.ANY)
    weight = pltpu.VMEM((D, D), BF16)
    dma = pltpu.SemaphoreType.DMA
    return pl.pallas_call(
        kernel,
        out_shape=pltpu.VMEM((MN, D), BF16),
        in_specs=[any_spec] * 14,
        out_specs=pl.BlockSpec(memory_space=pltpu.VMEM),
        scratch_shapes=[
            pltpu.VMEM((BR, D), BF16),
            pltpu.VMEM((1, BR), jnp.int32),
            pltpu.VMEM((BR // 128, 128), jnp.int32),
            weight,
            weight,
            pltpu.VMEM((GN, D), BF16),
            pltpu.VMEM((GN // 128, 128), jnp.int32),
            weight,
            weight,
            pltpu.VMEM((MN, D), BF16),
            pltpu.VMEM((NB, MN), jnp.int32),
            weight,
            weight,
            weight,
            pltpu.VMEM((NDEV, CAP, D), BF16),
            pltpu.VMEM((NDEV, 1, 128), F32),
            pltpu.VMEM((NDEV, CAP, D), BF16),
            pltpu.VMEM((NDEV, 1, 128), F32),
            pltpu.VMEM((3 * MN, D), F32),
            pltpu.VMEM((SLOTS, D), F32),
            pltpu.VMEM((SLOTS, D), F32),
            pltpu.VMEM((SLOTS, SLOTS), BF16),
            pltpu.VMEM((3 * MN, SLOTS), BF16),
            pltpu.VMEM((SLOTS, D), BF16),
            pltpu.VMEM((2, D // HALF, MN, HALF), BF16),
            pltpu.VMEM((2, D // HALF, MN, HALF), BF16),
            pltpu.VMEM((2 * H, D), BF16),
            pltpu.VMEM((MN, D), BF16),
            pltpu.VMEM((MN, MN), BF16),
            pltpu.VMEM((MN, 2 * H), BF16),
            dma((15,)),
            dma((NCHUNK,)),
            dma,
            dma,
            dma,
            dma,
            dma((2 * len(PIECES) * (D // HALF),)),
            dma((2 * len(PIECES) * (D // HALF),)),
            dma((2,)),
            dma((2,)),
            dma((2,)),
        ],
        compiler_params=pltpu.CompilerParams(
            collective_id=0, has_side_effects=True, vmem_limit_bytes=56 * 1024 * 1024
        ),
        name="fused",
    )(
        strip, owner.T, node.reshape(BR // 128, 128), d1, d2, feats, tgt.reshape(GN // 128, 128),
        e1, e2, init, nbrs.T, ps, pa, po,
    )


def solution(mesh):
    rows = P(("grp", "patch"), None)
    flat = P(("grp", "patch"))
    in_specs = (rows, rows, flat, P(), P(), rows, flat, P(), P(), rows, rows, P(), P(), P())
    return jax.shard_map(
        per_device, mesh=mesh, in_specs=in_specs, out_specs=rows, check_vma=False
    )
```

```python
import jax
import jax.numpy as jnp
from jax import lax
from jax.experimental import pallas as pl
from jax.experimental.pallas import tpu as pltpu
from jax.sharding import PartitionSpec as P

CAP = 8
NB = 6
H = 64
D = 512
GN = 4096
MN = 512
BR = 256
NDEV = 128
SLOTS = NDEV * CAP
CHUNK = 2048
NCHUNK = GN // CHUNK
HALF = 256
RUNS = ((0, 0, H), (MN - H, H, H), (H, 2 * H, MN - 2 * H))
PIECES = (((0, 2 * H), (2 * H, 320), (320, MN)), ((0, 2 * H), (2 * H, MN)))
MESH = pl.DeviceIdType.MESH
F32 = jnp.float32
BF16 = jnp.bfloat16

ORDER = sorted(
    [
        (dx, dy, dz, dc)
        for dx in range(4)
        for dy in range(4)
        for dz in range(4)
        for dc in range(2)
        if dx or dy or dz or dc
    ],
    key=lambda o: (-sum(min(v, 4 - v) for v in o[:3]), (o[0] + 2 * o[1] + 3 * o[2]) % 4, o),
)


def coords():
    g = lax.axis_index("grp")
    p = lax.axis_index("patch")
    return g, p // 8, (p // 2) % 4, p % 2


def shifted(at, offset):
    x, y, z, c = at
    dx, dy, dz, dc = offset
    xx = (x + dx) % 4 if dx else x
    yy = (y + dy) % 4 if dy else y
    zz = (z + dz) % 4 if dz else z
    cc = 1 - c if dc else c
    return xx, yy * 8 + zz * 2 + cc


def silu(v):
    half = v * 0.5
    return half + half * jnp.tanh(half)


def dot(a, b):
    return jnp.dot(a, b, preferred_element_type=F32)


def iota(shape, dim):
    return lax.broadcasted_iota(jnp.int32, shape, dim)


def onehot(mask):
    return jnp.where(mask, 1.0, 0.0).astype(BF16)


def col_to_row(col):
    n = col.shape[0]
    parts = []
    for b in range(n // 128):
        diag = iota((128, 128), 0) == iota((128, 128), 1)
        parts.append(
            jnp.sum(jnp.where(diag, col[b * 128 : (b + 1) * 128], 0.0), axis=0, keepdims=True)
        )
    return jnp.concatenate(parts, axis=1)


def kernel(
    strip, owner, node, d1, d2, feats, tgt, e1, e2, init, nbrs, ps, pa, po,
    out,
    strip_v, owner_v, node_v, d1_v, d2_v, feats_v, tgt_v, e1_v, e2_v, init_v, nbrs_v, ps_v, pa_v, po_v,
    send, nsend, recv, nrecv, sums, u_all, h_all, uj, hj, eq, tp, delta, xs, xr, hr, lat, c_own, c_halo,
    lsem, fsem, s_row, r_row, s_node, r_node, s_x, r_x, s_h, r_h, own_sem,
):
    at = coords()
    gi = lax.axis_index("grp")
    pi = lax.axis_index("patch")
    me = gi * 32 + pi

    loads = [
        pltpu.make_async_copy(src, dst, lsem.at[i])
        for i, (src, dst) in enumerate(
            [
                (owner, owner_v), (node, node_v), (strip, strip_v), (d1, d1_v), (d2, d2_v),
                (e1, e1_v), (tgt, tgt_v), (nbrs, nbrs_v), (e2, e2_v), (ps, ps_v), (pa, pa_v), (po, po_v),
            ]
            + [(init.at[pl.ds(src, n)], init_v.at[pl.ds(dst, n)]) for src, dst, n in RUNS]
        )
    ]

    def feat_load(c):
        rows = pl.ds(pl.multiple_of(c * CHUNK, CHUNK), CHUNK)
        return pltpu.make_async_copy(feats.at[rows], feats_v.at[rows], fsem.at[c])

    for c in loads[:6]:
        c.start()
    barrier = pltpu.get_barrier_semaphore()
    for o in ORDER:
        pl.semaphore_signal(barrier, inc=1, device_id=shifted(at, o), device_id_type=MESH)
    for c in range(NCHUNK):
        feat_load(c).start()
    for c in loads[6:]:
        c.start()

    loads[0].wait()
    loads[1].wait()
    owner_row = owner_v[...]
    node_row = jnp.concatenate([node_v[0:1, :], node_v[1:2, :]], axis=1).astype(F32)
    hit = iota((NDEV, BR), 0) == owner_row
    upper = onehot(iota((BR, BR), 0) < iota((BR, BR), 1))
    before = dot(onehot(hit), upper)
    slot_row = jnp.sum(jnp.where(hit, before, 0.0), axis=0, keepdims=True).astype(jnp.int32)
    pos_row = owner_row * CAP + slot_row
    placed = iota((SLOTS, BR), 0) == pos_row
    ncol = jnp.sum(jnp.where(placed, node_row + 1.0, 0.0), axis=1, keepdims=True) - 1.0
    ncol = jnp.broadcast_to(ncol.reshape(NDEV, CAP, 1), (NDEV, CAP, 128))
    pick = iota((NDEV, CAP, 128), 1) == iota((NDEV, CAP, 128), 2)
    nsend[...] = jnp.sum(jnp.where(pick, ncol, 0.0), axis=1, keepdims=True)

    for c in loads[2:6]:
        c.wait()
    hid = silu(dot(strip_v[...], d1_v[...])).astype(BF16)
    bnd = dot(hid, d2_v[...]).astype(BF16)
    rows_out = dot(bnd, e1_v[...]).astype(BF16)
    send[...] = dot(onehot(placed), rows_out).astype(BF16).reshape(NDEV, CAP, D)

    pl.semaphore_wait(barrier, NDEV - 1)
    for o in ORDER:
        to = shifted(at, o)
        idx = to[0] * 32 + to[1]
        pltpu.make_async_remote_copy(
            src_ref=nsend.at[idx], dst_ref=nrecv.at[me], send_sem=s_node, recv_sem=r_node,
            device_id=to, device_id_type=MESH,
        ).start()
    for o in ORDER:
        to = shifted(at, o)
        idx = to[0] * 32 + to[1]
        pltpu.make_async_remote_copy(
            src_ref=send.at[idx], dst_ref=recv.at[me], send_sem=s_row, recv_sem=r_row,
            device_id=to, device_id_type=MESH,
        ).start()
    own_n = pltpu.make_async_copy(nsend.at[me], nrecv.at[me], own_sem.at[0])
    own_r = pltpu.make_async_copy(send.at[me], recv.at[me], own_sem.at[1])
    own_n.start()
    own_r.start()

    for c in loads[6:]:
        c.wait()
    t_all = tgt_v[...]
    t_side, t_mesh = t_all // MN, t_all % MN
    t_mesh = jnp.where(
        t_mesh < H, t_mesh, jnp.where(t_mesh >= MN - H, t_mesh - (MN - 2 * H), t_mesh + H)
    )
    t_all = t_side * MN + t_mesh
    tgt_v[...] = t_all
    sums[:MN, :] = jnp.zeros((MN, D), F32)
    sums[2 * MN :, :] = jnp.zeros((MN, D), F32)

    def targets(c):
        first = c * (CHUNK // 128)
        return jnp.concatenate(
            [tgt_v[first + i : first + i + 1, :] for i in range(CHUNK // 128)], axis=1
        )

    def encode(c):
        feat_load(c).wait()
        rows = slice(c * CHUNK, (c + 1) * CHUNK)
        u = dot(feats_v[rows, :], e1_v[...])
        u_all[rows, :] = u.astype(BF16)
        h = silu(u).astype(BF16)
        h_all[rows, :] = h
        t_row = targets(c)
        for b in (0, 2):
            hot = onehot(iota((MN, CHUNK), 0) + b * MN == t_row)
            sums[b * MN : (b + 1) * MN, :] += dot(hot, h)

    for c in range(NCHUNK):
        encode(c)

    halo_lane = iota((MN, 2 * H), 1)
    halo_name = jnp.where(halo_lane < H, halo_lane, halo_lane + MN)
    lane = iota((MN, MN), 1)
    own_name = jnp.where(lane < H, lane + H, jnp.where(lane < 2 * H, lane + MN - H, lane))
    own_cnt = jnp.zeros((MN, MN), F32)
    halo_cnt = jnp.zeros((MN, 2 * H), F32)
    names = jnp.concatenate([nbrs_v[...].astype(F32), jnp.zeros((8 - NB, MN), F32)], axis=0)
    names = names.T.astype(jnp.int32)
    names = jnp.concatenate([names[src : src + n] for src, _, n in RUNS], axis=0)
    for k in range(NB):
        e = names[:, k : k + 1]
        own_cnt += jnp.where(e == own_name, 1.0, 0.0)
        halo_cnt += jnp.where(e == halo_name, 1.0, 0.0)
    c_own[...] = own_cnt.astype(BF16)
    c_halo[...] = halo_cnt.astype(BF16)

    all_n = pltpu.make_async_remote_copy(
        src_ref=nsend.at[pl.ds(0, NDEV - 1)], dst_ref=nrecv.at[pl.ds(0, NDEV - 1)],
        send_sem=s_node, recv_sem=r_node, device_id=(gi, pi), device_id_type=MESH,
    )
    all_n.wait_send()
    all_n.wait_recv()
    own_n.wait()
    got = jnp.broadcast_to(nrecv[...], (NDEV, CAP, 128))
    node_col = jnp.sum(jnp.where(pick, got, 0.0), axis=2, keepdims=True).reshape(SLOTS, 1)
    nrow = col_to_row(node_col)
    same = node_col == nrow
    eq[...] = onehot(same)
    earlier = iota((SLOTS, SLOTS), 0) < iota((SLOTS, SLOTS), 1)
    dup = jnp.sum(jnp.where(same & earlier, 1.0, 0.0), axis=0, keepdims=True)

    node_int = node_col.astype(jnp.int32)
    picked = jnp.zeros((SLOTS, D), F32)
    for c in range(NCHUNK):
        hot = onehot(iota((SLOTS, CHUNK), 1) + c * CHUNK == node_int)
        picked = picked + dot(hot, u_all[c * CHUNK : (c + 1) * CHUNK, :])
    uj[...] = picked
    hj[...] = silu(picked)

    hi_hot = onehot(iota((SLOTS, GN // 128), 1) == node_int // 128)
    t_hi = dot(hi_hot, (t_all // 64).astype(F32).astype(BF16))
    t_lo = dot(hi_hot, (t_all % 64).astype(F32).astype(BF16))
    t_val = t_hi * 64.0 + t_lo
    lane_pick = iota((SLOTS, 128), 1) == node_int % 128
    t_col = jnp.sum(jnp.where(lane_pick, t_val, 0.0), axis=1, keepdims=True)
    t_row = col_to_row(t_col)
    t_row = jnp.where((dup == 0.0) & (nrow >= 0.0), t_row, -1.0).astype(jnp.int32)
    for b in range(3):
        tp[b * MN : (b + 1) * MN, :] = onehot(iota((MN, SLOTS), 0) + b * MN == t_row)

    all_r = pltpu.make_async_remote_copy(
        src_ref=send.at[pl.ds(0, NDEV - 1)], dst_ref=recv.at[pl.ds(0, NDEV - 1)],
        send_sem=s_row, recv_sem=r_row, device_id=(gi, pi), device_id_type=MESH,
    )
    all_r.wait_send()
    all_r.wait_recv()
    own_r.wait()
    core = pi % 2
    peers = ((gi, (pi + 31 + 2 * core) % 32), (gi, pi + 1 - 2 * core))
    bases = (2 * MN * core, 2 * MN * (1 - core))
    copies = {}

    def send_sums(way, w, pieces):
        cols = slice(w * HALF, (w + 1) * HALF)
        lo, hi = PIECES[way][pieces[0]][0], PIECES[way][pieces[-1]][1]
        rows = pl.ds(pl.multiple_of(bases[way] + lo, H), hi - lo)
        xs[way, w, lo:hi, :] = (sums[rows, cols] + dot(tp[rows, :], delta[:, cols])).astype(BF16)
        for b in pieces:
            part = pl.ds(PIECES[way][b][0], PIECES[way][b][1] - PIECES[way][b][0])
            i = ((way * 2) + w) * 3 + b
            c = pltpu.make_async_remote_copy(
                src_ref=xs.at[way, w, part], dst_ref=xr.at[way, w, part],
                send_sem=s_x.at[i], recv_sem=r_x.at[i],
                device_id=peers[way], device_id_type=MESH,
            )
            c.start()
            copies[way, w, b] = c

    forced = [
        dot(eq[...], recv[:, :, w * HALF : (w + 1) * HALF].reshape(SLOTS, HALF))
        for w in range(D // HALF)
    ]
    for w in range(D // HALF):
        cols = slice(w * HALF, (w + 1) * HALF)
        delta[:, cols] = (silu(uj[:, cols] + forced[w]) - hj[:, cols]).astype(BF16)
        send_sums(0, w, (0,))
    for w in range(D // HALF):
        send_sums(1, w, (0,))
    for w in range(D // HALF):
        send_sums(0, w, (1, 2))
    for w in range(D // HALF):
        send_sums(1, w, (1,))

    def own_sums(lo, hi):
        acc = dot(tp[MN + lo : MN + hi, :], delta[...])
        for c in range(NCHUNK):
            hot = onehot(iota((hi - lo, CHUNK), 0) + (MN + lo) == targets(c))
            acc = acc + dot(hot, h_all[c * CHUNK : (c + 1) * CHUNK, :])
        sums[MN + lo : MN + hi, :] = acc

    own_sums(0, 2 * H)

    halo = [
        pltpu.make_async_remote_copy(
            src_ref=lat.at[pl.ds(pl.multiple_of(src, H), H)],
            dst_ref=hr.at[pl.ds(pl.multiple_of(H - src, H), H)],
            send_sem=s_h.at[i], recv_sem=r_h.at[i], device_id=peers[i], device_id_type=MESH,
        )
        for i, src in enumerate((H * core, H * (1 - core)))
    ]
    pre = jnp.zeros((MN, D), F32)
    parts = []
    for b, (lo, hi) in enumerate(PIECES[0]):
        for w in range(D // HALF):
            for way in range(2):
                if b < len(PIECES[way]):
                    copies[way, w, b].wait_recv()
        total = [
            (
                sums[MN + lo : MN + hi, w * HALF : (w + 1) * HALF]
                + xr[0, w, lo:hi, :].astype(F32)
                + xr[1, w, lo:hi, :].astype(F32)
            ).astype(BF16)
            for w in range(D // HALF)
        ]
        now = (
            init_v[lo:hi, :].astype(F32) + dot(jnp.concatenate(total, axis=1), e2_v[...])
        ).astype(BF16)
        lat[lo:hi, :] = now
        if b == 0:
            for c in halo:
                c.start()
            own_sums(2 * H, MN)
        parts.append(dot(now, ps_v[...]))
        pre = pre + dot(c_own[:, lo:hi], dot(now, pa_v[...]).astype(BF16))
    pre = pre + jnp.concatenate(parts, axis=0)
    for c in halo:
        c.wait_recv()
    pre = pre + dot(c_halo[...], dot(hr[...], pa_v[...]).astype(BF16))
    hidden = silu(pre).astype(BF16)
    new = (lat[...].astype(F32) + dot(hidden, po_v[...])).astype(BF16)
    for src, dst, n in RUNS:
        out[src : src + n, :] = new[dst : dst + n]
    for c in list(copies.values()) + halo:
        c.wait_send()


def per_device(strip, owner, node, d1, d2, feats, tgt, e1, e2, init, nbrs, ps, pa, po):
    any_spec = pl.BlockSpec(memory_space=pl.ANY)
    weight = pltpu.VMEM((D, D), BF16)
    dma = pltpu.SemaphoreType.DMA
    return pl.pallas_call(
        kernel,
        out_shape=pltpu.VMEM((MN, D), BF16),
        in_specs=[any_spec] * 14,
        out_specs=pl.BlockSpec(memory_space=pltpu.VMEM),
        scratch_shapes=[
            pltpu.VMEM((BR, D), BF16),
            pltpu.VMEM((1, BR), jnp.int32),
            pltpu.VMEM((BR // 128, 128), jnp.int32),
            weight,
            weight,
            pltpu.VMEM((GN, D), BF16),
            pltpu.VMEM((GN // 128, 128), jnp.int32),
            weight,
            weight,
            pltpu.VMEM((MN, D), BF16),
            pltpu.VMEM((NB, MN), jnp.int32),
            weight,
            weight,
            weight,
            pltpu.VMEM((NDEV, CAP, D), BF16),
            pltpu.VMEM((NDEV, 1, 128), F32),
            pltpu.VMEM((NDEV, CAP, D), BF16),
            pltpu.VMEM((NDEV, 1, 128), F32),
            pltpu.VMEM((3 * MN, D), F32),
            pltpu.VMEM((GN, D), BF16),
            pltpu.VMEM((GN, D), BF16),
            pltpu.VMEM((SLOTS, D), F32),
            pltpu.VMEM((SLOTS, D), F32),
            pltpu.VMEM((SLOTS, SLOTS), BF16),
            pltpu.VMEM((3 * MN, SLOTS), BF16),
            pltpu.VMEM((SLOTS, D), BF16),
            pltpu.VMEM((2, D // HALF, MN, HALF), BF16),
            pltpu.VMEM((2, D // HALF, MN, HALF), BF16),
            pltpu.VMEM((2 * H, D), BF16),
            pltpu.VMEM((MN, D), BF16),
            pltpu.VMEM((MN, MN), BF16),
            pltpu.VMEM((MN, 2 * H), BF16),
            dma((15,)),
            dma((NCHUNK,)),
            dma,
            dma,
            dma,
            dma,
            dma((12,)),
            dma((12,)),
            dma((2,)),
            dma((2,)),
            dma((2,)),
        ],
        compiler_params=pltpu.CompilerParams(
            collective_id=0, has_side_effects=True, vmem_limit_bytes=56 * 1024 * 1024
        ),
        name="fused",
    )(
        strip, owner.T, node.reshape(BR // 128, 128), d1, d2, feats, tgt.reshape(GN // 128, 128),
        e1, e2, init, nbrs.T, ps, pa, po,
    )


def solution(mesh):
    rows = P(("grp", "patch"), None)
    flat = P(("grp", "patch"))
    in_specs = (rows, rows, flat, P(), P(), rows, flat, P(), P(), rows, rows, P(), P(), P())
    return jax.shard_map(
        per_device, mesh=mesh, in_specs=in_specs, out_specs=rows, check_vma=False
    )
```

```python
import jax
import jax.numpy as jnp
from jax import lax
from jax.experimental import pallas as pl
from jax.experimental.pallas import tpu as pltpu
from jax.sharding import PartitionSpec as P

CAP = 8
NB = 6
H = 64
D = 512
GN = 4096
MN = 512
BR = 256
NDEV = 128
SLOTS = NDEV * CAP
CHUNK = 2048
NCHUNK = GN // CHUNK
HALF = 256
FIRST = 96
RUNS = ((0, 0, H), (MN - H, H, H), (H, 2 * H, MN - 2 * H))
PIECES = (((0, 2 * H), (2 * H, 320), (320, MN)), ((0, 2 * H), (2 * H, MN)))
MESH = pl.DeviceIdType.MESH
F32 = jnp.float32
BF16 = jnp.bfloat16

ORDER = sorted(
    [
        (dx, dy, dz, dc)
        for dx in range(4)
        for dy in range(4)
        for dz in range(4)
        for dc in range(2)
        if dx or dy or dz or dc
    ],
    key=lambda o: (-sum(min(v, 4 - v) for v in o[:3]), (o[0] + 2 * o[1] + 3 * o[2]) % 4, o),
)


def coords():
    g = lax.axis_index("grp")
    p = lax.axis_index("patch")
    return g, p // 8, (p // 2) % 4, p % 2


def shifted(at, offset):
    x, y, z, c = at
    dx, dy, dz, dc = offset
    xx = (x + dx) % 4 if dx else x
    yy = (y + dy) % 4 if dy else y
    zz = (z + dz) % 4 if dz else z
    cc = 1 - c if dc else c
    return xx, yy * 8 + zz * 2 + cc


def silu(v):
    half = v * 0.5
    return half + half * jnp.tanh(half)


def dot(a, b):
    return jnp.dot(a, b, preferred_element_type=F32)


def iota(shape, dim):
    return lax.broadcasted_iota(jnp.int32, shape, dim)


def onehot(mask):
    return jnp.where(mask, 1.0, 0.0).astype(BF16)


def col_to_row(col):
    n = col.shape[0]
    parts = []
    for b in range(n // 128):
        diag = iota((128, 128), 0) == iota((128, 128), 1)
        parts.append(
            jnp.sum(jnp.where(diag, col[b * 128 : (b + 1) * 128], 0.0), axis=0, keepdims=True)
        )
    return jnp.concatenate(parts, axis=1)


def kernel(
    strip, owner, node, d1, d2, feats, tgt, e1, e2, init, nbrs, ps, pa, po,
    out,
    strip_v, owner_v, node_v, d1_v, d2_v, feats_v, tgt_v, e1_v, e2_v, init_v, nbrs_v, ps_v, pa_v, po_v,
    send, nsend, recv, nrecv, sums, own, u_all, h_all, uj, hj, eq, tp, delta, xs, xr, hr, lat, c_own, c_halo,
    lsem, fsem, s_row, r_row, s_node, r_node, s_x, r_x, s_h, r_h, own_sem,
):
    at = coords()
    gi = lax.axis_index("grp")
    pi = lax.axis_index("patch")
    me = gi * 32 + pi

    loads = [
        pltpu.make_async_copy(src, dst, lsem.at[i])
        for i, (src, dst) in enumerate(
            [
                (owner, owner_v), (node, node_v), (strip, strip_v), (d1, d1_v), (d2, d2_v),
                (e1, e1_v), (tgt, tgt_v), (nbrs, nbrs_v), (e2, e2_v), (ps, ps_v), (pa, pa_v), (po, po_v),
            ]
            + [(init.at[pl.ds(src, n)], init_v.at[pl.ds(dst, n)]) for src, dst, n in RUNS]
        )
    ]

    def feat_load(c):
        rows = pl.ds(pl.multiple_of(c * CHUNK, CHUNK), CHUNK)
        return pltpu.make_async_copy(feats.at[rows], feats_v.at[rows], fsem.at[c])

    for c in loads[:6]:
        c.start()
    barrier = pltpu.get_barrier_semaphore()
    for o in ORDER:
        pl.semaphore_signal(barrier, inc=1, device_id=shifted(at, o), device_id_type=MESH)
    for c in range(NCHUNK):
        feat_load(c).start()
    for c in loads[6:]:
        c.start()

    loads[0].wait()
    loads[1].wait()
    owner_row = owner_v[...]
    node_row = jnp.concatenate([node_v[0:1, :], node_v[1:2, :]], axis=1).astype(F32)
    hit = iota((NDEV, BR), 0) == owner_row
    upper = onehot(iota((BR, BR), 0) < iota((BR, BR), 1))
    before = dot(onehot(hit), upper)
    slot_row = jnp.sum(jnp.where(hit, before, 0.0), axis=0, keepdims=True).astype(jnp.int32)
    pos_row = owner_row * CAP + slot_row
    placed = iota((SLOTS, BR), 0) == pos_row
    ncol = jnp.sum(jnp.where(placed, node_row + 1.0, 0.0), axis=1, keepdims=True) - 1.0
    ncol = jnp.broadcast_to(ncol.reshape(NDEV, CAP, 1), (NDEV, CAP, 128))
    pick = iota((NDEV, CAP, 128), 1) == iota((NDEV, CAP, 128), 2)
    nsend[...] = jnp.sum(jnp.where(pick, ncol, 0.0), axis=1, keepdims=True)

    for c in loads[2:6]:
        c.wait()
    hid = silu(dot(strip_v[...], d1_v[...])).astype(BF16)
    bnd = dot(hid, d2_v[...]).astype(BF16)
    rows_out = dot(bnd, e1_v[...]).astype(BF16)
    send[...] = dot(onehot(placed), rows_out).astype(BF16).reshape(NDEV, CAP, D)

    pl.semaphore_wait(barrier, NDEV - 1)
    for k, o in enumerate(ORDER):
        to = shifted(at, o)
        idx = to[0] * 32 + to[1]
        pltpu.make_async_remote_copy(
            src_ref=nsend.at[idx], dst_ref=nrecv.at[k], send_sem=s_node, recv_sem=r_node,
            device_id=to, device_id_type=MESH,
        ).start()
    for k, o in enumerate(ORDER):
        to = shifted(at, o)
        idx = to[0] * 32 + to[1]
        pltpu.make_async_remote_copy(
            src_ref=send.at[idx], dst_ref=recv.at[k], send_sem=s_row,
            recv_sem=r_row.at[0 if k < FIRST else 1], device_id=to, device_id_type=MESH,
        ).start()
    own_n = pltpu.make_async_copy(nsend.at[me], nrecv.at[NDEV - 1], own_sem.at[0])
    own_r = pltpu.make_async_copy(send.at[me], recv.at[NDEV - 1], own_sem.at[1])
    own_n.start()
    own_r.start()

    core = pi % 2
    peers = ((gi, (pi + 31 + 2 * core) % 32), (gi, pi + 1 - 2 * core))
    bases = (2 * MN * core, 2 * MN * (1 - core))

    for c in loads[6:]:
        c.wait()
    t_all = tgt_v[...]
    t_side, t_mesh = t_all // MN, t_all % MN
    t_mesh = jnp.where(
        t_mesh < H, t_mesh, jnp.where(t_mesh >= MN - H, t_mesh - (MN - 2 * H), t_mesh + H)
    )
    t_all = t_side * MN + t_mesh
    tgt_v[...] = t_all
    sums[...] = jnp.zeros_like(sums)

    def targets(c):
        first = c * (CHUNK // 128)
        return jnp.concatenate(
            [tgt_v[first + i : first + i + 1, :] for i in range(CHUNK // 128)], axis=1
        )

    def encode(c):
        feat_load(c).wait()
        rows = slice(c * CHUNK, (c + 1) * CHUNK)
        u = dot(feats_v[rows, :], e1_v[...])
        u_all[rows, :] = u.astype(BF16)
        h = silu(u).astype(BF16)
        h_all[rows, :] = h
        t_row = targets(c)
        sums[...] += dot(onehot(iota((MN, CHUNK), 0) + bases[0] == t_row), h)

    for c in range(NCHUNK):
        encode(c)

    halo_lane = iota((MN, 2 * H), 1)
    halo_name = jnp.where(halo_lane < H, halo_lane, halo_lane + MN)
    lane = iota((MN, MN), 1)
    own_name = jnp.where(lane < H, lane + H, jnp.where(lane < 2 * H, lane + MN - H, lane))
    own_cnt = jnp.zeros((MN, MN), F32)
    halo_cnt = jnp.zeros((MN, 2 * H), F32)
    names = jnp.concatenate([nbrs_v[...].astype(F32), jnp.zeros((8 - NB, MN), F32)], axis=0)
    names = names.T.astype(jnp.int32)
    names = jnp.concatenate([names[src : src + n] for src, _, n in RUNS], axis=0)
    for k in range(NB):
        e = names[:, k : k + 1]
        own_cnt += jnp.where(e == own_name, 1.0, 0.0)
        halo_cnt += jnp.where(e == halo_name, 1.0, 0.0)
    c_own[...] = own_cnt.astype(BF16)
    c_halo[...] = halo_cnt.astype(BF16)

    all_n = pltpu.make_async_remote_copy(
        src_ref=nsend.at[pl.ds(0, NDEV - 1)], dst_ref=nrecv.at[pl.ds(0, NDEV - 1)],
        send_sem=s_node, recv_sem=r_node, device_id=(gi, pi), device_id_type=MESH,
    )
    all_n.wait_send()
    all_n.wait_recv()
    own_n.wait()
    got = jnp.broadcast_to(nrecv[...], (NDEV, CAP, 128))
    node_col = jnp.sum(jnp.where(pick, got, 0.0), axis=2, keepdims=True).reshape(SLOTS, 1)
    nrow = col_to_row(node_col)
    same = node_col == nrow
    eq[...] = onehot(same)
    earlier = iota((SLOTS, SLOTS), 0) < iota((SLOTS, SLOTS), 1)
    dup = jnp.sum(jnp.where(same & earlier, 1.0, 0.0), axis=0, keepdims=True)

    node_int = node_col.astype(jnp.int32)
    picked = jnp.zeros((SLOTS, D), F32)
    for c in range(NCHUNK):
        hot = onehot(iota((SLOTS, CHUNK), 1) + c * CHUNK == node_int)
        picked = picked + dot(hot, u_all[c * CHUNK : (c + 1) * CHUNK, :])
    uj[...] = picked
    hj[...] = silu(picked)

    hi_hot = onehot(iota((SLOTS, GN // 128), 1) == node_int // 128)
    t_hi = dot(hi_hot, (t_all // 64).astype(F32).astype(BF16))
    t_lo = dot(hi_hot, (t_all % 64).astype(F32).astype(BF16))
    t_val = t_hi * 64.0 + t_lo
    lane_pick = iota((SLOTS, 128), 1) == node_int % 128
    t_col = jnp.sum(jnp.where(lane_pick, t_val, 0.0), axis=1, keepdims=True)
    t_row = col_to_row(t_col)
    t_row = jnp.where((dup == 0.0) & (nrow >= 0.0), t_row, -1.0).astype(jnp.int32)
    for b in range(3):
        tp[b * MN : (b + 1) * MN, :] = onehot(iota((MN, SLOTS), 0) + b * MN == t_row)

    def arrived(lo, hi, sem):
        return pltpu.make_async_remote_copy(
            src_ref=send.at[pl.ds(lo, hi - lo)], dst_ref=recv.at[pl.ds(lo, hi - lo)],
            send_sem=s_row, recv_sem=sem, device_id=(gi, pi), device_id_type=MESH,
        )

    def forcing(lo, hi, w):
        rows = recv[lo:hi, :, w * HALF : (w + 1) * HALF].reshape((hi - lo) * CAP, HALF)
        return dot(eq[:, lo * CAP : hi * CAP], rows)

    arrived(0, FIRST, r_row.at[0]).wait_recv()
    forced = [forcing(0, FIRST, w) for w in range(D // HALF)]
    arrived(0, NDEV - 1, r_row.at[0]).wait_send()
    arrived(FIRST, NDEV - 1, r_row.at[1]).wait_recv()
    own_r.wait()
    forced = [forced[w] + forcing(FIRST, NDEV, w) for w in range(D // HALF)]
    copies = {}

    def plain_sums(base, lo, hi):
        acc = dot(tp[pl.ds(pl.multiple_of(base + lo, H), hi - lo), :], delta[...])
        for c in range(NCHUNK):
            hot = onehot(iota((hi - lo, CHUNK), 0) + (base + lo) == targets(c))
            acc = acc + dot(hot, h_all[c * CHUNK : (c + 1) * CHUNK, :])
        return acc

    def send_sums(way, w, pieces):
        cols = slice(w * HALF, (w + 1) * HALF)
        lo, hi = PIECES[way][pieces[0]][0], PIECES[way][pieces[-1]][1]
        if way == 0:
            rows = pl.ds(pl.multiple_of(bases[0] + lo, H), hi - lo)
            xs[0, w, lo:hi, :] = (sums[lo:hi, cols] + dot(tp[rows, :], delta[:, cols])).astype(BF16)
        for b in pieces:
            part = pl.ds(PIECES[way][b][0], PIECES[way][b][1] - PIECES[way][b][0])
            i = ((way * 2) + w) * 3 + b
            c = pltpu.make_async_remote_copy(
                src_ref=xs.at[way, w, part], dst_ref=xr.at[way, w, part],
                send_sem=s_x.at[i], recv_sem=r_x.at[i],
                device_id=peers[way], device_id_type=MESH,
            )
            c.start()
            copies[way, w, b] = c

    for w in range(D // HALF):
        cols = slice(w * HALF, (w + 1) * HALF)
        delta[:, cols] = (silu(uj[:, cols] + forced[w]) - hj[:, cols]).astype(BF16)
        send_sums(0, w, (0,))
    for w in range(D // HALF):
        send_sums(0, w, (1, 2))

    for b, (lo, hi) in enumerate(PIECES[1]):
        part = plain_sums(bases[1], lo, hi).astype(BF16)
        for w in range(D // HALF):
            xs[1, w, lo:hi, :] = part[:, w * HALF : (w + 1) * HALF]
            send_sums(1, w, (b,))
    own[: 2 * H, :] = plain_sums(MN, 0, 2 * H)

    halo = [
        pltpu.make_async_remote_copy(
            src_ref=lat.at[pl.ds(pl.multiple_of(src, H), H)],
            dst_ref=hr.at[pl.ds(pl.multiple_of(H - src, H), H)],
            send_sem=s_h.at[i], recv_sem=r_h.at[i], device_id=peers[i], device_id_type=MESH,
        )
        for i, src in enumerate((H * core, H * (1 - core)))
    ]
    pre = jnp.zeros((MN, D), F32)
    parts = []
    for b, (lo, hi) in enumerate(PIECES[0]):
        for w in range(D // HALF):
            for way in range(2):
                if b < len(PIECES[way]):
                    copies[way, w, b].wait_recv()
        total = [
            (
                own[lo:hi, w * HALF : (w + 1) * HALF]
                + xr[0, w, lo:hi, :].astype(F32)
                + xr[1, w, lo:hi, :].astype(F32)
            ).astype(BF16)
            for w in range(D // HALF)
        ]
        now = (
            init_v[lo:hi, :].astype(F32) + dot(jnp.concatenate(total, axis=1), e2_v[...])
        ).astype(BF16)
        lat[lo:hi, :] = now
        if b == 0:
            for c in halo:
                c.start()
            own[2 * H :, :] = plain_sums(MN, 2 * H, MN)
        parts.append(dot(now, ps_v[...]))
        pre = pre + dot(c_own[:, lo:hi], dot(now, pa_v[...]).astype(BF16))
    pre = pre + jnp.concatenate(parts, axis=0)
    for c in halo:
        c.wait_recv()
    pre = pre + dot(c_halo[...], dot(hr[...], pa_v[...]).astype(BF16))
    hidden = silu(pre).astype(BF16)
    new = (lat[...].astype(F32) + dot(hidden, po_v[...])).astype(BF16)
    for src, dst, n in RUNS:
        out[src : src + n, :] = new[dst : dst + n]
    for c in list(copies.values()) + halo:
        c.wait_send()


def per_device(strip, owner, node, d1, d2, feats, tgt, e1, e2, init, nbrs, ps, pa, po):
    any_spec = pl.BlockSpec(memory_space=pl.ANY)
    weight = pltpu.VMEM((D, D), BF16)
    dma = pltpu.SemaphoreType.DMA
    return pl.pallas_call(
        kernel,
        out_shape=pltpu.VMEM((MN, D), BF16),
        in_specs=[any_spec] * 14,
        out_specs=pl.BlockSpec(memory_space=pltpu.VMEM),
        scratch_shapes=[
            pltpu.VMEM((BR, D), BF16),
            pltpu.VMEM((1, BR), jnp.int32),
            pltpu.VMEM((BR // 128, 128), jnp.int32),
            weight,
            weight,
            pltpu.VMEM((GN, D), BF16),
            pltpu.VMEM((GN // 128, 128), jnp.int32),
            weight,
            weight,
            pltpu.VMEM((MN, D), BF16),
            pltpu.VMEM((NB, MN), jnp.int32),
            weight,
            weight,
            weight,
            pltpu.VMEM((NDEV, CAP, D), BF16),
            pltpu.VMEM((NDEV, 1, 128), F32),
            pltpu.VMEM((NDEV, CAP, D), BF16),
            pltpu.VMEM((NDEV, 1, 128), F32),
            pltpu.VMEM((MN, D), F32),
            pltpu.VMEM((MN, D), F32),
            pltpu.VMEM((GN, D), BF16),
            pltpu.VMEM((GN, D), BF16),
            pltpu.VMEM((SLOTS, D), F32),
            pltpu.VMEM((SLOTS, D), F32),
            pltpu.VMEM((SLOTS, SLOTS), BF16),
            pltpu.VMEM((3 * MN, SLOTS), BF16),
            pltpu.VMEM((SLOTS, D), BF16),
            pltpu.VMEM((2, D // HALF, MN, HALF), BF16),
            pltpu.VMEM((2, D // HALF, MN, HALF), BF16),
            pltpu.VMEM((2 * H, D), BF16),
            pltpu.VMEM((MN, D), BF16),
            pltpu.VMEM((MN, MN), BF16),
            pltpu.VMEM((MN, 2 * H), BF16),
            dma((15,)),
            dma((NCHUNK,)),
            dma,
            dma((2,)),
            dma,
            dma,
            dma((12,)),
            dma((12,)),
            dma((2,)),
            dma((2,)),
            dma((2,)),
        ],
        compiler_params=pltpu.CompilerParams(
            collective_id=0, has_side_effects=True, vmem_limit_bytes=56 * 1024 * 1024
        ),
        name="fused",
    )(
        strip, owner.T, node.reshape(BR // 128, 128), d1, d2, feats, tgt.reshape(GN // 128, 128),
        e1, e2, init, nbrs.T, ps, pa, po,
    )


def solution(mesh):
    rows = P(("grp", "patch"), None)
    flat = P(("grp", "patch"))
    in_specs = (rows, rows, flat, P(), P(), rows, flat, P(), P(), rows, rows, P(), P(), P())
    return jax.shard_map(
        per_device, mesh=mesh, in_specs=in_specs, out_specs=rows, check_vma=False
    )
```

```python
import jax
import jax.numpy as jnp
from jax import lax
from jax.experimental import pallas as pl
from jax.experimental.pallas import tpu as pltpu
from jax.sharding import PartitionSpec as P

CAP = 8
NB = 6
H = 64
D = 512
GN = 4096
MN = 512
BR = 256
NDEV = 128
SLOTS = NDEV * CAP
CHUNK = 2048
NCHUNK = GN // CHUNK
HALF = 256
FIRST = 96
RUNS = ((0, 0, H), (MN - H, H, H), (H, 2 * H, MN - 2 * H))
PIECES = (((0, 2 * H), (2 * H, 320), (320, MN)), ((0, 2 * H), (2 * H, MN)))
MESH = pl.DeviceIdType.MESH
F32 = jnp.float32
BF16 = jnp.bfloat16

ORDER = sorted(
    [
        (dx, dy, dz, dc)
        for dx in range(4)
        for dy in range(4)
        for dz in range(4)
        for dc in range(2)
        if dx or dy or dz or dc
    ],
    key=lambda o: (-sum(min(v, 4 - v) for v in o[:3]), (o[0] + 2 * o[1] + 3 * o[2]) % 4, o),
)


def coords():
    g = lax.axis_index("grp")
    p = lax.axis_index("patch")
    return g, p // 8, (p // 2) % 4, p % 2


def shifted(at, offset):
    x, y, z, c = at
    dx, dy, dz, dc = offset
    xx = (x + dx) % 4 if dx else x
    yy = (y + dy) % 4 if dy else y
    zz = (z + dz) % 4 if dz else z
    cc = 1 - c if dc else c
    return xx, yy * 8 + zz * 2 + cc


def silu(v):
    half = v * 0.5
    return half + half * jnp.tanh(half)


def dot(a, b):
    return jnp.dot(a, b, preferred_element_type=F32)


def iota(shape, dim):
    return lax.broadcasted_iota(jnp.int32, shape, dim)


def onehot(mask):
    return jnp.where(mask, 1.0, 0.0).astype(BF16)


def col_to_row(col):
    n = col.shape[0]
    parts = []
    for b in range(n // 128):
        diag = iota((128, 128), 0) == iota((128, 128), 1)
        parts.append(
            jnp.sum(jnp.where(diag, col[b * 128 : (b + 1) * 128], 0.0), axis=0, keepdims=True)
        )
    return jnp.concatenate(parts, axis=1)


def kernel(
    strip, owner, node, d1, d2, feats, tgt, e1, e2, init, nbrs, ps, pa, po,
    out,
    strip_v, owner_v, node_v, d1_v, d2_v, feats_v, tgt_v, e1_v, e2_v, init_v, nbrs_v, ps_v, pa_v, po_v,
    send, nsend, recv, nrecv, sums, own, u_all, h_all, uj, hj, eq, tp, delta, xs, xr, hr, lat, c_own, c_halo,
    lsem, fsem, s_row, r_row, s_node, r_node, s_x, r_x, s_h, r_h, own_sem,
):
    at = coords()
    gi = lax.axis_index("grp")
    pi = lax.axis_index("patch")
    me = gi * 32 + pi

    loads = [
        pltpu.make_async_copy(src, dst, lsem.at[i])
        for i, (src, dst) in enumerate(
            [
                (owner, owner_v), (node, node_v), (strip, strip_v), (d1, d1_v), (d2, d2_v),
                (e1, e1_v), (tgt, tgt_v), (nbrs, nbrs_v), (e2, e2_v), (ps, ps_v), (pa, pa_v), (po, po_v),
            ]
            + [(init.at[pl.ds(src, n)], init_v.at[pl.ds(dst, n)]) for src, dst, n in RUNS]
        )
    ]

    def feat_load(c):
        rows = pl.ds(pl.multiple_of(c * CHUNK, CHUNK), CHUNK)
        return pltpu.make_async_copy(feats.at[rows], feats_v.at[rows], fsem.at[c])

    for c in loads[:6]:
        c.start()
    barrier = pltpu.get_barrier_semaphore()
    for o in ORDER:
        pl.semaphore_signal(barrier, inc=1, device_id=shifted(at, o), device_id_type=MESH)
    for c in range(NCHUNK):
        feat_load(c).start()
    for c in loads[6:]:
        c.start()

    loads[0].wait()
    loads[1].wait()
    owner_row = owner_v[...]
    node_row = jnp.concatenate([node_v[0:1, :], node_v[1:2, :]], axis=1).astype(F32)
    hit = iota((NDEV, BR), 0) == owner_row
    upper = onehot(iota((BR, BR), 0) < iota((BR, BR), 1))
    before = dot(onehot(hit), upper)
    slot_row = jnp.sum(jnp.where(hit, before, 0.0), axis=0, keepdims=True).astype(jnp.int32)
    pos_row = owner_row * CAP + slot_row
    placed = iota((SLOTS, BR), 0) == pos_row
    ncol = jnp.sum(jnp.where(placed, node_row + 1.0, 0.0), axis=1, keepdims=True) - 1.0
    ncol = jnp.broadcast_to(ncol.reshape(NDEV, CAP, 1), (NDEV, CAP, 128))
    pick = iota((NDEV, CAP, 128), 1) == iota((NDEV, CAP, 128), 2)
    nsend[...] = jnp.sum(jnp.where(pick, ncol, 0.0), axis=1, keepdims=True)

    for c in loads[2:6]:
        c.wait()
    hid = silu(dot(strip_v[...], d1_v[...])).astype(BF16)
    bnd = dot(hid, d2_v[...]).astype(BF16)
    rows_out = dot(bnd, e1_v[...]).astype(BF16)
    send[...] = dot(onehot(placed), rows_out).astype(BF16).reshape(NDEV, CAP, D)

    pl.semaphore_wait(barrier, NDEV - 1)
    for k, o in enumerate(ORDER):
        to = shifted(at, o)
        idx = to[0] * 32 + to[1]
        pltpu.make_async_remote_copy(
            src_ref=nsend.at[idx], dst_ref=nrecv.at[k], send_sem=s_node, recv_sem=r_node,
            device_id=to, device_id_type=MESH,
        ).start()
    for k, o in enumerate(ORDER):
        to = shifted(at, o)
        idx = to[0] * 32 + to[1]
        pltpu.make_async_remote_copy(
            src_ref=send.at[idx], dst_ref=recv.at[k], send_sem=s_row,
            recv_sem=r_row.at[0 if k < FIRST else 1], device_id=to, device_id_type=MESH,
        ).start()
    own_n = pltpu.make_async_copy(nsend.at[me], nrecv.at[NDEV - 1], own_sem.at[0])
    own_r = pltpu.make_async_copy(send.at[me], recv.at[NDEV - 1], own_sem.at[1])
    own_n.start()
    own_r.start()

    core = pi % 2
    peers = ((gi, (pi + 31 + 2 * core) % 32), (gi, pi + 1 - 2 * core))
    bases = (2 * MN * core, 2 * MN * (1 - core))

    for c in loads[6:]:
        c.wait()
    t_all = tgt_v[...]
    t_side, t_mesh = t_all // MN, t_all % MN
    t_mesh = jnp.where(
        t_mesh < H, t_mesh, jnp.where(t_mesh >= MN - H, t_mesh - (MN - 2 * H), t_mesh + H)
    )
    t_all = t_side * MN + t_mesh
    tgt_v[...] = t_all
    sums[...] = jnp.zeros_like(sums)

    def targets(c):
        first = c * (CHUNK // 128)
        return jnp.concatenate(
            [tgt_v[first + i : first + i + 1, :] for i in range(CHUNK // 128)], axis=1
        )

    def encode(c):
        feat_load(c).wait()
        rows = slice(c * CHUNK, (c + 1) * CHUNK)
        u = dot(feats_v[rows, :], e1_v[...])
        u_all[rows, :] = u.astype(BF16)
        h = silu(u).astype(BF16)
        h_all[rows, :] = h
        t_row = targets(c)
        sums[...] += dot(onehot(iota((MN, CHUNK), 0) + bases[0] == t_row), h)

    for c in range(NCHUNK):
        encode(c)

    halo_lane = iota((MN, 2 * H), 1)
    halo_name = jnp.where(halo_lane < H, halo_lane, halo_lane + MN)
    lane = iota((MN, MN), 1)
    own_name = jnp.where(lane < H, lane + H, jnp.where(lane < 2 * H, lane + MN - H, lane))
    own_cnt = jnp.zeros((MN, MN), F32)
    halo_cnt = jnp.zeros((MN, 2 * H), F32)
    names = jnp.concatenate([nbrs_v[...].astype(F32), jnp.zeros((8 - NB, MN), F32)], axis=0)
    names = names.T.astype(jnp.int32)
    names = jnp.concatenate([names[src : src + n] for src, _, n in RUNS], axis=0)
    for k in range(NB):
        e = names[:, k : k + 1]
        own_cnt += jnp.where(e == own_name, 1.0, 0.0)
        halo_cnt += jnp.where(e == halo_name, 1.0, 0.0)
    c_own[...] = own_cnt.astype(BF16)
    c_halo[...] = halo_cnt.astype(BF16)

    all_n = pltpu.make_async_remote_copy(
        src_ref=nsend.at[pl.ds(0, NDEV - 1)], dst_ref=nrecv.at[pl.ds(0, NDEV - 1)],
        send_sem=s_node, recv_sem=r_node, device_id=(gi, pi), device_id_type=MESH,
    )
    all_n.wait_send()
    all_n.wait_recv()
    own_n.wait()
    got = jnp.broadcast_to(nrecv[...], (NDEV, CAP, 128))
    node_col = jnp.sum(jnp.where(pick, got, 0.0), axis=2, keepdims=True).reshape(SLOTS, 1)
    nrow = col_to_row(node_col)
    same = node_col == nrow
    eq[...] = onehot(same)
    earlier = iota((SLOTS, SLOTS), 0) < iota((SLOTS, SLOTS), 1)
    dup = jnp.sum(jnp.where(same & earlier, 1.0, 0.0), axis=0, keepdims=True)

    node_int = node_col.astype(jnp.int32)
    picked = jnp.zeros((SLOTS, D), F32)
    for c in range(NCHUNK):
        hot = onehot(iota((SLOTS, CHUNK), 1) + c * CHUNK == node_int)
        picked = picked + dot(hot, u_all[c * CHUNK : (c + 1) * CHUNK, :])
    uj[...] = picked
    hj[...] = silu(picked)

    hi_hot = onehot(iota((SLOTS, GN // 128), 1) == node_int // 128)
    t_hi = dot(hi_hot, (t_all // 64).astype(F32).astype(BF16))
    t_lo = dot(hi_hot, (t_all % 64).astype(F32).astype(BF16))
    t_val = t_hi * 64.0 + t_lo
    lane_pick = iota((SLOTS, 128), 1) == node_int % 128
    t_col = jnp.sum(jnp.where(lane_pick, t_val, 0.0), axis=1, keepdims=True)
    t_row = col_to_row(t_col)
    t_row = jnp.where((dup == 0.0) & (nrow >= 0.0), t_row, -1.0).astype(jnp.int32)
    for b in range(3):
        tp[b * MN : (b + 1) * MN, :] = onehot(iota((MN, SLOTS), 0) + b * MN == t_row)

    def arrived(lo, hi, sem):
        return pltpu.make_async_remote_copy(
            src_ref=send.at[pl.ds(lo, hi - lo)], dst_ref=recv.at[pl.ds(lo, hi - lo)],
            send_sem=s_row, recv_sem=sem, device_id=(gi, pi), device_id_type=MESH,
        )

    def forcing(lo, hi, w):
        rows = recv[lo:hi, :, w * HALF : (w + 1) * HALF].reshape((hi - lo) * CAP, HALF)
        return dot(eq[:, lo * CAP : hi * CAP], rows)

    arrived(0, FIRST, r_row.at[0]).wait_recv()
    forced = [forcing(0, FIRST, w) for w in range(D // HALF)]
    arrived(0, NDEV - 1, r_row.at[0]).wait_send()
    arrived(FIRST, NDEV - 1, r_row.at[1]).wait_recv()
    own_r.wait()
    forced = [forced[w] + forcing(FIRST, NDEV, w) for w in range(D // HALF)]
    copies = {}

    def plain_sums(base, lo, hi):
        acc = dot(tp[pl.ds(pl.multiple_of(base + lo, H), hi - lo), :], delta[...])
        for c in range(NCHUNK):
            hot = onehot(iota((hi - lo, CHUNK), 0) + (base + lo) == targets(c))
            acc = acc + dot(hot, h_all[c * CHUNK : (c + 1) * CHUNK, :])
        return acc

    def send_sums(way, w, pieces):
        cols = slice(w * HALF, (w + 1) * HALF)
        lo, hi = PIECES[way][pieces[0]][0], PIECES[way][pieces[-1]][1]
        if way == 0:
            rows = pl.ds(pl.multiple_of(bases[0] + lo, H), hi - lo)
            xs[0, w, lo:hi, :] = (sums[lo:hi, cols] + dot(tp[rows, :], delta[:, cols])).astype(BF16)
        for b in pieces:
            part = pl.ds(PIECES[way][b][0], PIECES[way][b][1] - PIECES[way][b][0])
            i = ((way * 2) + w) * 3 + b
            c = pltpu.make_async_remote_copy(
                src_ref=xs.at[way, w, part], dst_ref=xr.at[way, w, part],
                send_sem=s_x.at[i], recv_sem=r_x.at[i],
                device_id=peers[way], device_id_type=MESH,
            )
            c.start()
            copies[way, w, b] = c

    for w in range(D // HALF):
        cols = slice(w * HALF, (w + 1) * HALF)
        delta[:, cols] = (silu(uj[:, cols] + forced[w]) - hj[:, cols]).astype(BF16)
        send_sums(0, w, (0,))
    for w in range(D // HALF):
        send_sums(0, w, (1, 2))

    for b, (lo, hi) in enumerate(PIECES[1]):
        if b == 1:
            own[: 2 * H, :] = plain_sums(MN, 0, 2 * H)
        part = plain_sums(bases[1], lo, hi).astype(BF16)
        for w in range(D // HALF):
            xs[1, w, lo:hi, :] = part[:, w * HALF : (w + 1) * HALF]
            send_sums(1, w, (b,))
    halo = [
        pltpu.make_async_remote_copy(
            src_ref=lat.at[pl.ds(pl.multiple_of(src, H), H)],
            dst_ref=hr.at[pl.ds(pl.multiple_of(H - src, H), H)],
            send_sem=s_h.at[i], recv_sem=r_h.at[i], device_id=peers[i], device_id_type=MESH,
        )
        for i, src in enumerate((H * core, H * (1 - core)))
    ]
    pre = jnp.zeros((MN, D), F32)
    parts = []
    for b, (lo, hi) in enumerate(PIECES[0]):
        for w in range(D // HALF):
            for way in range(2):
                if b < len(PIECES[way]):
                    copies[way, w, b].wait_recv()
        total = [
            (
                own[lo:hi, w * HALF : (w + 1) * HALF]
                + xr[0, w, lo:hi, :].astype(F32)
                + xr[1, w, lo:hi, :].astype(F32)
            ).astype(BF16)
            for w in range(D // HALF)
        ]
        now = (
            init_v[lo:hi, :].astype(F32) + dot(jnp.concatenate(total, axis=1), e2_v[...])
        ).astype(BF16)
        lat[lo:hi, :] = now
        if b == 0:
            for c in halo:
                c.start()
            own[2 * H :, :] = plain_sums(MN, 2 * H, MN)
        parts.append(dot(now, ps_v[...]))
        pre = pre + dot(c_own[:, lo:hi], dot(now, pa_v[...]).astype(BF16))
    pre = pre + jnp.concatenate(parts, axis=0)
    for c in halo:
        c.wait_recv()
    pre = pre + dot(c_halo[...], dot(hr[...], pa_v[...]).astype(BF16))
    hidden = silu(pre).astype(BF16)
    new = (lat[...].astype(F32) + dot(hidden, po_v[...])).astype(BF16)
    for src, dst, n in RUNS:
        out[src : src + n, :] = new[dst : dst + n]
    for c in list(copies.values()) + halo:
        c.wait_send()


def per_device(strip, owner, node, d1, d2, feats, tgt, e1, e2, init, nbrs, ps, pa, po):
    any_spec = pl.BlockSpec(memory_space=pl.ANY)
    weight = pltpu.VMEM((D, D), BF16)
    dma = pltpu.SemaphoreType.DMA
    return pl.pallas_call(
        kernel,
        out_shape=pltpu.VMEM((MN, D), BF16),
        in_specs=[any_spec] * 14,
        out_specs=pl.BlockSpec(memory_space=pltpu.VMEM),
        scratch_shapes=[
            pltpu.VMEM((BR, D), BF16),
            pltpu.VMEM((1, BR), jnp.int32),
            pltpu.VMEM((BR // 128, 128), jnp.int32),
            weight,
            weight,
            pltpu.VMEM((GN, D), BF16),
            pltpu.VMEM((GN // 128, 128), jnp.int32),
            weight,
            weight,
            pltpu.VMEM((MN, D), BF16),
            pltpu.VMEM((NB, MN), jnp.int32),
            weight,
            weight,
            weight,
            pltpu.VMEM((NDEV, CAP, D), BF16),
            pltpu.VMEM((NDEV, 1, 128), F32),
            pltpu.VMEM((NDEV, CAP, D), BF16),
            pltpu.VMEM((NDEV, 1, 128), F32),
            pltpu.VMEM((MN, D), F32),
            pltpu.VMEM((MN, D), F32),
            pltpu.VMEM((GN, D), BF16),
            pltpu.VMEM((GN, D), BF16),
            pltpu.VMEM((SLOTS, D), F32),
            pltpu.VMEM((SLOTS, D), F32),
            pltpu.VMEM((SLOTS, SLOTS), BF16),
            pltpu.VMEM((3 * MN, SLOTS), BF16),
            pltpu.VMEM((SLOTS, D), BF16),
            pltpu.VMEM((2, D // HALF, MN, HALF), BF16),
            pltpu.VMEM((2, D // HALF, MN, HALF), BF16),
            pltpu.VMEM((2 * H, D), BF16),
            pltpu.VMEM((MN, D), BF16),
            pltpu.VMEM((MN, MN), BF16),
            pltpu.VMEM((MN, 2 * H), BF16),
            dma((15,)),
            dma((NCHUNK,)),
            dma,
            dma((2,)),
            dma,
            dma,
            dma((12,)),
            dma((12,)),
            dma((2,)),
            dma((2,)),
            dma((2,)),
        ],
        compiler_params=pltpu.CompilerParams(
            collective_id=0, has_side_effects=True, vmem_limit_bytes=56 * 1024 * 1024
        ),
        name="fused",
    )(
        strip, owner.T, node.reshape(BR // 128, 128), d1, d2, feats, tgt.reshape(GN // 128, 128),
        e1, e2, init, nbrs.T, ps, pa, po,
    )


def solution(mesh):
    rows = P(("grp", "patch"), None)
    flat = P(("grp", "patch"))
    in_specs = (rows, rows, flat, P(), P(), rows, flat, P(), P(), rows, rows, P(), P(), P())
    return jax.shard_map(
        per_device, mesh=mesh, in_specs=in_specs, out_specs=rows, check_vma=False
    )
```
